128 devices in a mesh: basis: 64 (over y_hi, z, x, core), grp: 2 (over y_lo).
Axes of the slice: x: 4, y: 4 (y_hi: 2, y_lo: 2; y = y_hi * 2 + y_lo), z: 4, core: 2. Of those that a mesh axis runs over, the one named last changes fastest.
Arguments:
- bra: bfloat16 [262144, 4096], P('basis', 'grp'), may hold values from -0.01171875 to 0.01171875
- dipole: bfloat16 [2048, 8, 128, 128], P('basis'), may hold values from -6 to 6
- block_cols: int32 [2048, 8], P('basis'), may hold values from 0 to 2047, as said below
- ket: bfloat16 [262144, 512], P('basis', 'grp'), may hold values from -0.1875 to 0.1875
- j_upper: int32 [4096], P('grp'), may hold values from 0 to 6
- sym_upper: int32 [4096], P('grp'), may hold values from 0 to 1
- j_lower: int32 [512], replicated, may hold values from 0 to 6
- sym_lower: int32 [512], replicated, may hold values from 0 to 1
Outputs:
- strength: float32 [512, 4096], P('basis', 'grp')
The draws below stay inside these ranges and needn't reach their ends.
Inputs may be any that keep to these rules, and one draw needn't show every extreme that they name: block_cols[r, 0] = r, and every entry lies within 8 of its row r; entries of one row differ except where clipped to the range's ends.
All inputs are finite; a program needn't handle non-finite values.
Results may differ from the reference program's by a relative error of at most 0.0033.
Values may be sent and summed in bfloat16 or wider, within the bound.
A program may use at most 128 MiB of HBM per device.

```python
import jax
import jax.numpy as jnp
from jax import lax

BASIS = 262144
BLK = 128
NNZ = 8
REACH = 8
LOWER = 512
UPPER = 4096
BROWS = 2048


def draw_block_cols(key, part):
    key = jax.random.fold_in(key, 7)
    count = BASIS // BLK
    keys = jax.random.split(key, count)
    offsets = jnp.concatenate([jnp.arange(-REACH, 0), jnp.arange(1, REACH + 1)]).astype(jnp.int32)

    def one_row(row_key):
        return jax.random.permutation(row_key, offsets)[:NNZ - 1]
    picked = jax.vmap(one_row)(keys)
    picked = jnp.concatenate([jnp.zeros((count, 1), jnp.int32), picked], axis=1)
    rows = jnp.arange(count, dtype=jnp.int32)[:, None]
    return jnp.clip(rows + picked, 0, count - 1).astype(jnp.int32)


def touch_ends(result, key, low, largest):
    shape = result.shape
    place = [jax.random.randint(jax.random.fold_in(key, axis), (), 0, shape[axis]) for axis in range(len(shape))]
    result = result.at[tuple(place)].set(low)
    longest = shape.index(max(shape))
    place[longest] = (place[longest] + 1) % shape[longest]
    return result.at[tuple(place)].set(largest)


def levels(key, shape, cuts, least, high):
    def one(dim, parts):
        steps = jax.random.uniform(jax.random.fold_in(jax.random.fold_in(key, 6), dim), (parts,), jnp.float32, least / len(cuts), high / len(cuts))
        return jnp.repeat(jnp.exp(steps), shape[dim] // parts).reshape((-1,) + (1,) * (len(shape) - dim - 1))

    level = one(*cuts[0])
    for cut in cuts[1:]:
        level = level * one(*cut)
    return level


def centred(key, dims, spread, limit, pieces=(), kind=jnp.bfloat16):
    array = jax.random.normal(key, dims, jnp.float32) * spread
    if len(pieces) > 0:
        array = levels(key, dims, pieces, -0.22, 0.18) * array
    return jnp.clip(array, min=-limit, max=limit).astype(kind)


def setup_inputs(seed: int = 0) -> dict:
    arg_keys = jax.random.split(jax.random.key(seed), 9)
    return {
        "bra": centred(arg_keys[0], (BASIS, UPPER), BASIS ** -0.5, 0.01171875, ((0, 64), (1, 2))),
        "dipole": centred(arg_keys[1], (BROWS, NNZ, BLK, BLK), 1.0, 6.0, ((0, 64),)),
        "block_cols": draw_block_cols(jax.random.fold_in(arg_keys[8], 71), 0),
        "ket": centred(arg_keys[3], (BASIS, LOWER), (NNZ * BLK) ** -0.5, 0.1875, ((0, 64), (1, 2))),
        "j_upper": touch_ends(jax.random.randint(arg_keys[4], (UPPER,), 0, 7), jax.random.fold_in(arg_keys[4], 1), 0, 6).astype(jnp.int32),
        "sym_upper": touch_ends(jax.random.randint(arg_keys[5], (UPPER,), 0, 2), jax.random.fold_in(arg_keys[5], 1), 0, 1).astype(jnp.int32),
        "j_lower": touch_ends(jax.random.randint(arg_keys[6], (LOWER,), 0, 7), jax.random.fold_in(arg_keys[6], 1), 0, 6).astype(jnp.int32),
        "sym_lower": touch_ends(jax.random.randint(arg_keys[7], (LOWER,), 0, 2), jax.random.fold_in(arg_keys[7], 1), 0, 1).astype(jnp.int32),
    }


def reference(bra, dipole, block_cols, ket, j_upper, sym_upper, j_lower, sym_lower):
    count = BASIS // BLK
    ket_blocks = ket.reshape(count, BLK, LOWER)

    def block_rows(pair):
        blocks, columns = pair
        picked = ket_blocks[columns].astype(jnp.float32)
        return jnp.einsum("rkij,rkjp->rip", blocks.astype(jnp.float32), picked)

    applied = lax.map(block_rows, (dipole.reshape(count // 8, 8, NNZ, BLK, BLK), block_cols.reshape(count // 8, 8, NNZ)))
    applied = applied.reshape(BASIS, LOWER).astype(jnp.bfloat16)
    moment = lax.dot_general(applied, bra, (((0,), (0,)), ((), ())), preferred_element_type=jnp.float32)
    allowed = (jnp.abs(j_lower[:, None] - j_upper[None, :]) <= 1) & (sym_lower[:, None] != sym_upper[None, :])
    return jnp.where(allowed, moment * moment, jnp.zeros_like(moment))
```

```python
import jax
import jax.numpy as jnp
from jax import lax
from jax.experimental import pallas as pl
from jax.experimental.pallas import tpu as pltpu
from jax.sharding import PartitionSpec as P

MESH = pl.DeviceIdType.MESH
F32 = jnp.float32
BF16 = jnp.bfloat16

REACH = 8
BLK = 128
PLANE = 32
SEG = 16
NT = 256

CHUNKS = ((0, 4), (4, 2), (6, 1), (7, 1))


def pieces_of(chunk):
    if chunk == 0:
        return ((8, 4), (12, 4), (16, 4), (20, 4), (0, 4), (4, 4), (24, 4), (28, 4))
    return ((8, 8), (16, 8), (0, 8), (24, 8))


PIECES = tuple((c, r0, n) for c in range(len(CHUNKS)) for r0, n in pieces_of(c))
DIP_ROWS = 4
DIP_ORDER = (2, 3, 4, 5, 0, 1, 6, 7)


def kernel(
    cols, jl, sl, ju, su, bra_hbm, dip_hbm, ket_hbm, out,
    bra, dip, ket_own, ket_ext, perm, app_own, app_oth, stage,
    sb_own, rb_own, sb0, rb0, sb1, rb1, sb2, rb2, sb3, rb3,
    sum_own, sum_oth, sum_in,
    bra_sem, dip_sem, ket_sem, halo_send, halo_recv, y_send, y_recv, a_send, a_recv, s_send, s_recv,
):
    b = lax.axis_index("basis")
    g = lax.axis_index("grp")
    yh = b // PLANE
    me = b % PLANE
    nbr = dip_hbm.shape[0]
    last = 2 * PLANE - 1
    mine = yh == g

    ket_copies = [
        pltpu.make_async_copy(ket_hbm, ket_own, ket_sem.at[0]),
        pltpu.make_async_copy(ket_hbm, ket_ext.at[pl.ds(REACH, nbr)], ket_sem.at[1]),
    ]
    dip_copies = {}
    for i in DIP_ORDER:
        rows = pl.ds(i * DIP_ROWS, DIP_ROWS)
        dip_copies[i] = pltpu.make_async_copy(dip_hbm.at[rows], dip.at[rows], dip_sem.at[i])
    bra_copies = [
        pltpu.make_async_copy(bra_hbm.at[:, pl.ds(n * NT, NT)], bra.at[n], bra_sem.at[n])
        for n in range(bra.shape[0])
    ]
    ket_copies[0].start()
    for i in DIP_ORDER[:4]:
        dip_copies[i].start()
    ket_copies[1].start()
    for i in DIP_ORDER[4:]:
        dip_copies[i].start()
    for copy in bra_copies:
        copy.start()

    barrier = pltpu.get_barrier_semaphore()

    def greet(s, carry):
        peer = yh * PLANE + lax.rem(me + s, PLANE)
        pl.semaphore_signal(barrier, inc=1, device_id=(peer, g), device_id_type=MESH)
        return carry

    lax.fori_loop(1, PLANE, greet, 0)
    across = ((1 - yh) * PLANE + me, g)
    partner = (b, 1 - g)
    pl.semaphore_signal(barrier, inc=1, device_id=across, device_id_type=MESH)
    pl.semaphore_signal(barrier, inc=1, device_id=partner, device_id_type=MESH)

    @pl.when(b == PLANE - 1)
    def _():
        pl.semaphore_signal(barrier, inc=1, device_id=(PLANE, g), device_id_type=MESH)

    @pl.when(b == PLANE)
    def _():
        pl.semaphore_signal(barrier, inc=1, device_id=(PLANE - 1, g), device_id_type=MESH)

    size = perm.shape[0]
    place = lax.broadcasted_iota(jnp.int32, (size, size), 0)
    state = lax.broadcasted_iota(jnp.int32, (size, size), 1)
    wanted = (place & (PLANE - 1)) * 8 + (place >> 5)
    perm[...] = jnp.where(state == wanted, 1.0, 0.0).astype(BF16)

    pl.semaphore_wait(barrier, PLANE + 1 + jnp.where((b == PLANE - 1) | (b == PLANE), 1, 0))

    to_next = pltpu.make_async_remote_copy(
        ket_hbm.at[pl.ds(nbr - REACH, REACH)], ket_ext.at[pl.ds(0, REACH)],
        halo_send.at[0], halo_recv.at[0], device_id=(jnp.minimum(b + 1, last), g), device_id_type=MESH,
    )
    to_prev = pltpu.make_async_remote_copy(
        ket_hbm.at[pl.ds(0, REACH)], ket_ext.at[pl.ds(REACH + nbr, REACH)],
        halo_send.at[1], halo_recv.at[1], device_id=(jnp.maximum(b - 1, 0), g), device_id_type=MESH,
    )

    @pl.when(b < last)
    def _():
        to_next.start()

    @pl.when(b > 0)
    def _():
        to_prev.start()

    y_copies = []
    for i, (c, r0, n) in enumerate(PIECES):
        e0, ne = CHUNKS[c]
        part = (pl.ds(e0 * PLANE, ne * PLANE), pl.ds(r0 * BLK, n * BLK))
        y_copies.append(
            pltpu.make_async_remote_copy(
                app_own.at[part], app_oth.at[part], y_send.at[i], y_recv.at[i],
                device_id=partner, device_id_type=MESH,
            )
        )

    def apply_rows(r0, n, ket, base):
        def one(i, carry):
            r = r0 + i
            top = ket.shape[0] - 1
            blocks = [ket[jnp.clip(cols[r, k] - base, 0, top)] for k in range(cols.shape[1])]
            row = jnp.concatenate([dip[r, k] for k in range(cols.shape[1])], axis=1)
            value = jnp.dot(row, jnp.concatenate(blocks, axis=0), preferred_element_type=F32)
            turned = lax.dot_general(
                perm[...], value.astype(BF16), (((1,), (1,)), ((), ())), preferred_element_type=F32
            )
            app_own[:, pl.ds(pl.multiple_of(r * BLK, BLK), BLK)] = turned.astype(BF16)
            return carry

        lax.fori_loop(0, n, one, 0)

    ket_copies[0].wait()
    for i, (c, r0, n) in enumerate(PIECES):
        if c > 0:
            y_copies[i].start()
            continue
        dip_copies[r0 // DIP_ROWS].wait()
        if i == 4:
            ket_copies[1].wait()

            @pl.when(b > 0)
            def _():
                to_next.wait_recv()

            @pl.when(b < last)
            def _():
                to_prev.wait_recv()

        if REACH <= r0 and r0 + n <= nbr - REACH:
            apply_rows(r0, n, ket_own, b * nbr)
        else:
            apply_rows(r0, n, ket_ext, b * nbr - REACH)
        y_copies[i].start()

    def contract(lhs, e0, ne, k0, kw, add):
        rows = ne * PLANE

        def one(n, carry):
            value = jnp.dot(
                lhs[pl.ds(e0 * PLANE, rows), pl.ds(k0, kw)], bra[n, pl.ds(k0, kw), :],
                preferred_element_type=F32,
            )
            for h in range(NT // 128):
                for q in range(rows // 8):
                    e, o = q // (PLANE // 8), (q % (PLANE // 8)) * 8
                    at = pl.ds(o * SEG * ne + e * SEG + n * (NT // 128) + h, 8, stride=SEG * ne)
                    tile = value[q * 8:q * 8 + 8, h * 128:h * 128 + 128]
                    if add:
                        tile = stage[at, :] + tile
                    stage[at, :] = tile
            return carry

        lax.fori_loop(0, bra.shape[0], one, 0)

    def scatter(ne, sb, rb, sem):
        rows = ne * SEG

        def cast(o, carry):
            at = pl.ds(pl.multiple_of(o * 4 * rows, 4 * rows), 4 * rows)
            sb[at, :] = stage[at, :].astype(BF16)
            return carry

        lax.fori_loop(0, PLANE // 4, cast, 0)

        def send(s, carry):
            owner = lax.rem(me + s, PLANE)
            pltpu.make_async_remote_copy(
                sb.at[pl.ds(pl.multiple_of(owner * rows, rows), rows)],
                rb.at[pl.ds(pl.multiple_of(s * rows, rows), rows)],
                a_send.at[sem], a_recv.at[sem],
                device_id=(yh * PLANE + owner, g), device_id_type=MESH,
            ).start()
            return carry

        lax.fori_loop(1, PLANE, send, 0)

    def gather(ne, sb, rb, sem, total, e0):
        rows = ne * SEG
        pltpu.make_async_remote_copy(
            sb.at[pl.ds(0, (PLANE - 1) * rows)], rb.at[pl.ds(rows, (PLANE - 1) * rows)],
            a_send.at[sem], a_recv.at[sem], device_id=partner, device_id_type=MESH,
        ).wait()

        def one(s, value):
            return value + rb[pl.ds(pl.multiple_of(s * rows, rows), rows), :].astype(F32)

        value = sb[pl.ds(pl.multiple_of(me * rows, rows), rows), :].astype(F32)
        total[pl.ds(e0 * SEG, rows), :] = lax.fori_loop(1, PLANE, one, value)

    def hop(total, e0, ne, sem):
        part = pl.ds(e0 * SEG, ne * SEG)
        return pltpu.make_async_remote_copy(
            total.at[part], sum_in.at[part], s_send.at[sem], s_recv.at[sem],
            device_id=across, device_id_type=MESH,
        )

    for copy in bra_copies:
        copy.wait()
    contract(app_own, 0, 8, 0, nbr * BLK, False)
    scatter(8, sb_own, rb_own, 4)

    boxes = ((sb0, rb0), (sb1, rb1), (sb2, rb2), (sb3, rb3))
    hop_own = hop(sum_own, 0, 8, 4)
    hops = [hop(sum_oth, e0, ne, c) for c, (e0, ne) in enumerate(CHUNKS)]

    def finish(c):
        e0, ne = CHUNKS[c]
        gather(ne, *boxes[c], c, sum_oth, e0)

        @pl.when(mine)
        def _():
            hops[c].start()

    for c, (e0, ne) in enumerate(CHUNKS):
        first = True
        todo = [(y_copies[i], r0, n) for i, (cc, r0, n) in enumerate(PIECES) if cc == c]
        if c < len(CHUNKS) - 1:
            for copy, _, _ in todo:
                copy.wait_recv()
            contract(app_oth, e0, ne, 0, nbr * BLK, False)
        else:
            for copy, r0, n in todo:
                copy.wait_recv()
                contract(app_oth, e0, ne, r0 * BLK, n * BLK, not first)
                first = False
        scatter(ne, *boxes[c], c)
        if c == 0:
            gather(8, sb_own, rb_own, 4, sum_own, 0)

            @pl.when(jnp.logical_not(mine))
            def _():
                hop_own.start()
        else:
            finish(c - 1)
    finish(len(CHUNKS) - 1)

    @pl.when(mine)
    def _():
        hop_own.wait_recv()
        sum_in[...] = sum_in[...] + sum_own[...]

    @pl.when(jnp.logical_not(mine))
    def _():
        for copy in hops:
            copy.wait_recv()
        sum_in[...] = sum_in[...] + sum_oth[...]

    for e in range(8):
        j = jl[8 * b + e]
        s = sl[8 * b + e]
        at = pl.ds(e * SEG, SEG)
        value = sum_in[at, :]
        allowed = (jnp.abs(j - ju[...]) <= 1) & (su[...] != s)
        stage[at, :] = jnp.where(allowed, value * value, jnp.zeros_like(value))
    for t in range(SEG):
        out[:, t * 128:t * 128 + 128] = stage[pl.ds(t, 8, stride=SEG), :]

    for copy in y_copies:
        copy.wait_send()

    @pl.when(b < last)
    def _():
        to_next.wait_send()

    @pl.when(b > 0)
    def _():
        to_prev.wait_send()

    @pl.when(mine)
    def _():
        for copy in hops:
            copy.wait_send()

    @pl.when(jnp.logical_not(mine))
    def _():
        hop_own.wait_send()


def on_device(bra, dipole, block_cols, ket, j_upper, sym_upper, j_lower, sym_lower):
    rows, upper = bra.shape
    half = ket.shape[1]
    nbr = rows // BLK
    vmem = pl.BlockSpec(memory_space=pltpu.VMEM)
    smem = pl.BlockSpec(memory_space=pltpu.SMEM)
    hbm = pl.BlockSpec(memory_space=pl.ANY)
    box = lambda ne: pltpu.VMEM((PLANE * ne * SEG, 128), BF16)
    boxes = [box(8)] * 2
    for _, ne in CHUNKS:
        boxes += [box(ne)] * 2
    dma = lambda n: pltpu.SemaphoreType.DMA((n,))
    flops = 2 * rows * 8 * BLK * half + 2 * rows * 2 * half * upper
    return pl.pallas_call(
        kernel,
        out_shape=jax.ShapeDtypeStruct((8, upper), F32),
        in_specs=[smem, smem, smem, vmem, vmem, hbm, hbm, hbm],
        out_specs=vmem,
        scratch_shapes=[
            pltpu.VMEM((upper // NT, rows, NT), BF16),
            pltpu.VMEM(dipole.shape, BF16),
            pltpu.VMEM((nbr, BLK, half), BF16),
            pltpu.VMEM((nbr + 2 * REACH, BLK, half), BF16),
            pltpu.VMEM((half, half), BF16),
            pltpu.VMEM((half, rows), BF16),
            pltpu.VMEM((half, rows), BF16),
            pltpu.VMEM((half * SEG, 128), F32),
            *boxes,
            pltpu.VMEM((8 * SEG, 128), F32),
            pltpu.VMEM((8 * SEG, 128), F32),
            pltpu.VMEM((8 * SEG, 128), F32),
            dma(upper // NT), dma(nbr // DIP_ROWS), dma(2), dma(2), dma(2),
            dma(len(PIECES)), dma(len(PIECES)), dma(5), dma(5), dma(5), dma(5),
        ],
        compiler_params=pltpu.CompilerParams(
            collective_id=0, has_side_effects=True, vmem_limit_bytes=56 * 1024 * 1024
        ),
        cost_estimate=pl.CostEstimate(flops=flops, bytes_accessed=28 * 1024 * 1024, transcendentals=0),
    )(
        block_cols, j_lower, sym_lower,
        j_upper.reshape(upper // 128, 128), sym_upper.reshape(upper // 128, 128),
        bra, dipole, ket.reshape(nbr, BLK, half),
    )


def solution(mesh):
    return jax.shard_map(
        on_device,
        mesh=mesh,
        in_specs=(
            P("basis", "grp"),
            P("basis", None, None, None),
            P("basis", None),
            P("basis", "grp"),
            P("grp"),
            P("grp"),
            P(),
            P(),
        ),
        out_specs=P("basis", "grp"),
        check_vma=False,
    )
```

```python
import jax
import jax.numpy as jnp
from jax import lax
from jax.experimental import pallas as pl
from jax.experimental.pallas import tpu as pltpu
from jax.sharding import PartitionSpec as P

MESH = pl.DeviceIdType.MESH
F32 = jnp.float32
BF16 = jnp.bfloat16

REACH = 8
BLK = 128
PLANE = 32
LINE = 8
SEG = 16
NT = 512

CHIPS = PLANE // 2
SHIFTS = sorted(
    ((dx, dz) for dz in range(4) for dx in range(4) if dx or dz),
    key=lambda t: -min(t[0], 4 - t[0]) - min(t[1], 4 - t[1]),
)
CHUNKS = ((0, 4), (4, 2), (6, 1), (7, 1))
LAST = len(CHUNKS) - 1
PIECES = (
    (0, 8, 4), (0, 12, 4), (0, 16, 4), (0, 20, 4), (1, 8, 16),
    (0, 0, 8), (0, 24, 8), (1, 0, 8), (1, 24, 8),
    (2, 8, 16), (2, 0, 8), (2, 24, 8),
    (3, 8, 16), (3, 0, 8), (3, 24, 4), (3, 28, 4),
)
DIP_ROWS = 4
ARRIVALS = (
    (0, 8, 16), (1, 8, 16), (0, 0, 8), (0, 24, 8), (1, 0, 8), (1, 24, 8),
    (2, 8, 16), (2, 0, 8), (2, 24, 8), (3, 8, 16), (3, 0, 8), (3, 24, 4), (3, 28, 4),
)
INNER = ((8, (0,)), (12, (1,)), (16, (2,)), (20, (3, 4)))
OUTER = ((0, ()), (4, (5,)), (24, ()), (28, (6, 7, 8, 9, 10, 11, 12, 13, 14, 15)))
STEPS = INNER + OUTER
RELAY = 10


def kernel(
    cols_hbm, jl_hbm, sl_hbm, ju_hbm, su_hbm, bra_hbm, dip_hbm, ket_hbm, out,
    cols, jl, sl, ju, su,
    bra, dip, ket_own, ket_ext, relay, perm, app_own, app_oth, mask,
    acc_own, acc0, acc1, acc2, acc3,
    stage_own, stage0, stage1, stage2, stage3, pair_own, pair0, pair1, pair2,
    sb_own, rb_own, sb0, rb0, sb1, rb1, sb2, rb2, sb3, rb3,
    sum_own, sum_oth, sum_in,
    small_sem, bra_sem, dip_sem, ket_sem, halo_send, halo_recv, corner_send, corner_recv,
    y_send, y_recv, pair_send, pair_recv, a_send, a_recv, s_send, s_recv, round_sem,
):
    b = lax.axis_index("basis")
    g = lax.axis_index("grp")
    yh = b // PLANE
    me = b % PLANE
    nbr = dip_hbm.shape[0]
    last = 2 * PLANE - 1
    low, high = PLANE - 1, PLANE
    mine = yh == g
    theirs = yh != g
    across = ((1 - yh) * PLANE + me, g)
    partner = (b, 1 - g)

    def tell(sem, device):
        pl.semaphore_signal(sem, inc=1, device_id=device, device_id_type=MESH)

    barrier = pltpu.get_barrier_semaphore()
    tell(barrier, partner)
    tell(barrier, across)
    for s in range(1, LINE):
        tell(barrier, (yh * PLANE + (me ^ s), g))
    for s in range(1, PLANE // LINE):
        tell(barrier, (yh * PLANE + (me ^ (s * LINE)), g))

    small = [
        pltpu.make_async_copy(src, dst, small_sem.at[i])
        for i, (src, dst) in enumerate(((cols_hbm, cols), (jl_hbm, jl), (sl_hbm, sl), (ju_hbm, ju), (su_hbm, su)))
    ]
    ket_copies = [
        pltpu.make_async_copy(ket_hbm, ket_own, ket_sem.at[0]),
        pltpu.make_async_copy(ket_hbm, ket_ext.at[pl.ds(REACH, nbr)], ket_sem.at[1]),
    ]
    dip_copies = {}
    for i, (r0, _) in enumerate(STEPS):
        rows = pl.ds(r0, DIP_ROWS)
        dip_copies[r0] = pltpu.make_async_copy(dip_hbm.at[rows], dip.at[rows], dip_sem.at[i])
    bra_copies = [
        pltpu.make_async_copy(bra_hbm.at[:, pl.ds(n * NT, NT)], bra.at[n], bra_sem.at[n])
        for n in range(bra.shape[0])
    ]
    small[0].start()
    ket_copies[0].start()
    for r0, _ in STEPS[:4]:
        dip_copies[r0].start()
    ket_copies[1].start()
    for r0, _ in STEPS[4:]:
        dip_copies[r0].start()
    @pl.when(me > 0)
    def _():
        tell(barrier, (b - 1, g))

    @pl.when(me < low)
    def _():
        tell(barrier, (b + 1, g))

    at_low, at_high = b == low, b == high
    relays_up = [high + RELAY * j for j in (1, 2, 3)]
    relays_down = [RELAY * j for j in (0, 1, 2)]
    is_up = (b == relays_up[0]) | (b == relays_up[1]) | (b == relays_up[2])
    is_down = (b == relays_down[0]) | (b == relays_down[1]) | (b == relays_down[2])

    @pl.when(at_low)
    def _():
        for peer in [high] + relays_up + relays_down:
            tell(barrier, (peer, g))

    @pl.when(at_high)
    def _():
        for peer in [low] + relays_up + relays_down:
            tell(barrier, (peer, g))

    @pl.when(is_up | is_down)
    def _():
        tell(barrier, (low, g))
        tell(barrier, (high, g))

    size = perm.shape[0]
    place = lax.broadcasted_iota(jnp.int32, (size, size), 0)
    state = lax.broadcasted_iota(jnp.int32, (size, size), 1)
    region = place & (PLANE - 1)
    wanted = (2 * (region & (CHIPS - 1)) + region // CHIPS) * 8 + place // PLANE
    perm[...] = jnp.where(state == wanted, 1.0, 0.0).astype(BF16)

    def apply_rows(r0, n, ket, base):
        def one(i, carry):
            r = r0 + i
            top = ket.shape[0] - 1
            blocks = [ket[jnp.clip(cols[k, r] - base, 0, top)] for k in range(cols.shape[0])]
            row = jnp.concatenate([dip[r, k] for k in range(cols.shape[0])], axis=1)
            value = jnp.dot(row, jnp.concatenate(blocks, axis=0), preferred_element_type=F32)
            turned = lax.dot_general(
                perm[...], value.astype(BF16), (((1,), (1,)), ((), ())), preferred_element_type=F32
            )
            app_own[:, pl.ds(pl.multiple_of(r * BLK, BLK), BLK)] = turned.astype(BF16)
            return carry

        lax.fori_loop(0, n, one, 0)

    def to_next(dst):
        return pltpu.make_async_remote_copy(
            ket_hbm.at[pl.ds(nbr - REACH, REACH)], ket_ext.at[pl.ds(0, REACH)],
            halo_send.at[0], halo_recv.at[0], device_id=(dst, g), device_id_type=MESH,
        )

    def to_prev(dst):
        return pltpu.make_async_remote_copy(
            ket_hbm.at[pl.ds(0, REACH)], ket_ext.at[pl.ds(REACH + nbr, REACH)],
            halo_send.at[1], halo_recv.at[1], device_id=(dst, g), device_id_type=MESH,
        )

    next_copy, prev_copy = to_next(jnp.minimum(b + 1, last)), to_prev(jnp.maximum(b - 1, 0))
    quarter = REACH // 4

    def corner(src, dst, sem, device):
        return pltpu.make_async_remote_copy(
            src, dst, corner_send.at[sem], corner_recv.at[sem], device_id=(device, g), device_id_type=MESH
        )

    def ket_part(start, j):
        return ket_hbm.at[pl.ds(start + quarter * j, quarter)]

    def ext_part(start, j):
        return ket_ext.at[pl.ds(start + quarter * j, quarter)]

    up_first = [corner(ket_part(nbr - REACH, 0), ext_part(0, 0), 0, high)]
    up_first += [corner(ket_part(nbr - REACH, j), relay, j, high + RELAY * j) for j in (1, 2, 3)]
    up_second = [corner(relay, ext_part(0, j), j, high) for j in (1, 2, 3)]
    down_first = [corner(ket_part(0, 3), ext_part(REACH + nbr, 3), 3, low)]
    down_first += [corner(ket_part(0, j), relay, j, RELAY * j) for j in (0, 1, 2)]
    down_second = [corner(relay, ext_part(REACH + nbr, j), j, low) for j in (0, 1, 2)]

    def relay_on():
        for j in (1, 2, 3):
            @pl.when(b == high + RELAY * j)
            def _():
                up_first[j].wait_recv()
                up_second[j - 1].start()
        for j in (0, 1, 2):
            @pl.when(b == RELAY * j)
            def _():
                down_first[j + 1].wait_recv()
                down_second[j].start()

    def halo_wait():
        ket_copies[1].wait()

        @pl.when((b > 0) & (b != high))
        def _():
            next_copy.wait_recv()

        @pl.when((b < last) & (b != low))
        def _():
            prev_copy.wait_recv()

        @pl.when(at_high)
        def _():
            up_first[0].wait_recv()
            for copy in up_second:
                copy.wait_recv()

        @pl.when(at_low)
        def _():
            down_first[0].wait_recv()
            for copy in down_second:
                copy.wait_recv()

    y_copies = []
    for i, (c, r0, n) in enumerate(PIECES):
        e0, ne = CHUNKS[c]
        part = (pl.ds(e0 * PLANE, ne * PLANE), pl.ds(r0 * BLK, n * BLK))
        y_copies.append(
            pltpu.make_async_remote_copy(
                app_own.at[part], app_oth.at[part], y_send.at[i], y_recv.at[i],
                device_id=partner, device_id_type=MESH,
            )
        )

    def enter():
        many = jnp.where(at_low | at_high, 7, jnp.where(is_up | is_down, 2, 0))
        ends = jnp.where(me > 0, 1, 0) + jnp.where(me < low, 1, 0)
        pl.semaphore_wait(barrier, LINE + PLANE // LINE + ends + many)

        @pl.when((b < last) & (b != low))
        def _():
            next_copy.start()

        @pl.when((b > 0) & (b != high))
        def _():
            prev_copy.start()

        @pl.when(at_low)
        def _():
            for copy in up_first:
                copy.start()

        @pl.when(at_high)
        def _():
            for copy in down_first:
                copy.start()

    def apply_step(r0, ready, ket, base):
        dip_copies[r0].wait()
        apply_rows(r0, DIP_ROWS, ket, base)
        if r0 == INNER[0][0]:
            enter()
        for k in ready:
            y_copies[k].start()

    def spread(value, stage, ne, first):
        for h in range(value.shape[1] // 128):
            for q in range(value.shape[0] // 8):
                e, o = q // (PLANE // 8), (q % (PLANE // 8)) * 8
                at = pl.ds(o * SEG * ne + e * SEG + first + h, 8, stride=SEG * ne)
                stage[at, :] = value[q * 8:q * 8 + 8, h * 128:h * 128 + 128]

    def contract(lhs, acc, stage, e0, ne, r0, n, begin, end):
        k = pl.ds(r0 * BLK, n * BLK)

        def one(t, carry):
            value = jnp.dot(
                lhs[pl.ds(e0 * PLANE, ne * PLANE), k], bra[t, k, :], preferred_element_type=F32
            )
            if not begin:
                value = value + acc[t]
            if end:
                spread(value, stage, ne, t * (NT // 128))
            else:
                acc[t] = value
            return carry

        if ne > 2:
            lax.fori_loop(0, bra.shape[0], one, 0)
        else:
            for t in range(bra.shape[0]):
                one(t, 0)

    core = me & 1
    chip = me // 2

    def meet(ne, stage, pair, sem):
        rows = CHIPS * ne * SEG
        theirs_at = pl.ds(pl.multiple_of((1 - core) * rows, rows), rows)
        return pltpu.make_async_remote_copy(
            stage.at[theirs_at], pair, pair_send.at[sem], pair_recv.at[sem],
            device_id=(b ^ 1, g), device_id_type=MESH,
        )

    def scatter(ne, stage, pair, sb, rb, sem):
        rows = ne * SEG
        meet(ne, stage, pair, sem).wait()

        def one(o, carry):
            at = pl.ds(pl.multiple_of(o * 4 * rows, 4 * rows), 4 * rows)
            own = pl.ds(pl.multiple_of(core * CHIPS * rows + o * 4 * rows, 4 * rows), 4 * rows)
            sb[at, :] = (stage[own, :] + pair[at, :]).astype(BF16)
            return carry

        lax.fori_loop(0, CHIPS // 4, one, 0)
        for slot, (dx, dz) in enumerate(SHIFTS):
            owner = (chip // 4 + dz) % 4 * 4 + (chip % 4 + dx) % 4
            pltpu.make_async_remote_copy(
                sb.at[pl.ds(pl.multiple_of(owner * rows, rows), rows)], rb.at[pl.ds(slot * rows, rows)],
                a_send.at[sem], a_recv.at[sem],
                device_id=(yh * PLANE + 2 * owner + core, g), device_id_type=MESH,
            ).start()

    def take(ne, sb, rb, sem, total, e0):
        rows = ne * SEG
        pltpu.make_async_remote_copy(
            sb.at[pl.ds(0, (CHIPS - 1) * rows)], rb, a_send.at[sem], a_recv.at[sem],
            device_id=partner, device_id_type=MESH,
        ).wait()
        add_up(ne, sb, chip, rb, CHIPS - 1, total, e0)

    def add_up(ne, sb, region, rb, slots, total, e0):
        rows = ne * SEG

        def one(s, value):
            return value + rb[pl.ds(pl.multiple_of(s * rows, rows), rows), :].astype(F32)

        value = sb[pl.ds(pl.multiple_of(region * rows, rows), rows), :].astype(F32)
        total[pl.ds(e0 * SEG, rows), :] = lax.fori_loop(0, slots, one, value)

    def scatter_last(ne, stage, sb, rb, plane, begin, slot, sem):
        rows = ne * SEG

        def send(s, carry):
            owner = lax.rem(me + s, PLANE)
            region = (owner & 1) * CHIPS + owner // 2
            pltpu.make_async_remote_copy(
                sb.at[pl.ds(pl.multiple_of(region * rows, rows), rows)],
                rb.at[pl.ds(pl.multiple_of((slot + s - begin) * rows, rows), rows)],
                a_send.at[sem], a_recv.at[sem],
                device_id=(plane * PLANE + owner, g), device_id_type=MESH,
            ).start()
            return carry

        lax.fori_loop(begin, PLANE, send, 0)

    def all_of(ne, sb, rb, begin, slot, sem):
        rows = ne * SEG
        return pltpu.make_async_remote_copy(
            sb.at[pl.ds(0, (PLANE - begin) * rows)], rb.at[pl.ds(slot * rows, (PLANE - begin) * rows)],
            a_send.at[sem], a_recv.at[sem], device_id=partner, device_id_type=MESH,
        )

    def hop(total, e0, ne, sem):
        part = pl.ds(e0 * SEG, ne * SEG)
        return pltpu.make_async_remote_copy(
            total.at[part], sum_in.at[part], s_send.at[sem], s_recv.at[sem],
            device_id=across, device_id_type=MESH,
        )

    OWN = LAST + 1
    hop_own = hop(sum_own, 0, 8, OWN)
    hops = [hop(sum_oth, e0, ne, c) for c, (e0, ne) in enumerate(CHUNKS[:LAST])]
    boxes = ((sb0, rb0), (sb1, rb1), (sb2, rb2))
    stages = (stage0, stage1, stage2, stage3)
    pairs = (pair0, pair1, pair2)

    def finish(c):
        e0, ne = CHUNKS[c]
        take(ne, *boxes[c], c, sum_oth, e0)

        @pl.when(mine)
        def _():
            hops[c].start()

    def main():
        small[0].wait()
        ket_copies[0].wait()
        for r0, ready in INNER:
            apply_step(r0, ready, ket_own, b * nbr)
            if r0 == INNER[1][0]:
                for s in range(1, PLANE // LINE):
                    tell(round_sem.at[0], (yh * PLANE + (me ^ (s * LINE)), g))
        for copy in bra_copies:
            copy.start()
        for copy in small[1:]:
            copy.start()
        relay_on()
        for copy in bra_copies:
            copy.wait()
        contract(app_own, acc_own, stage_own, 0, 8, REACH, nbr - 2 * REACH, True, False)
        pl.semaphore_wait(round_sem.at[0], PLANE // LINE - 1)
        tell(round_sem.at[1], across)
        halo_wait()
        for r0, ready in OUTER:
            apply_step(r0, ready, ket_ext, b * nbr - REACH)
        contract(app_own, acc_own, stage_own, 0, 8, 0, REACH, False, False)
        contract(app_own, acc_own, stage_own, 0, 8, nbr - REACH, REACH, False, True)
        meet(8, stage_own, pair_own, OWN).start()
        pl.semaphore_wait(round_sem.at[1], 1)

    main()

    def rules():
        for copy in small[1:]:
            copy.wait()
        for e in range(8):
            allowed = (jnp.abs(jl[8 * b + e] - ju[...]) <= 1) & (su[...] != sl[8 * b + e])
            mask[pl.ds(e * SEG, SEG), :] = jnp.where(allowed, 1.0, 0.0)

    def finish_own():
        take(8, sb_own, rb_own, OWN, sum_own, 0)

        @pl.when(theirs)
        def _():
            hop_own.start()

    accs = (acc0, acc1, acc2, acc3)
    seen = [0] * len(CHUNKS)
    for i, (c, r0, n) in enumerate(ARRIVALS):
        e0, ne = CHUNKS[c]
        for copy, (cc, p0, m) in zip(y_copies, PIECES):
            if cc == c and r0 <= p0 and p0 + m <= r0 + n:
                copy.wait_recv()
        full = seen[c] + n == nbr
        contract(app_oth, accs[c], stages[c], e0, ne, r0, n, seen[c] == 0, full)
        seen[c] += n
        if full and c < LAST:
            meet(ne, stages[c], pairs[c], c).start()
        if i == 0:
            scatter(8, stage_own, pair_own, sb_own, rb_own, OWN)
        if i == 3:
            finish_own()
        if i == 5:
            rules()
        if i == 8:
            finish(1)
        if full and c < LAST:
            scatter(ne, stages[c], pairs[c], *boxes[c], c)
        if i == 6:
            finish(0)
    e0, ne = CHUNKS[LAST]
    for q in range(4):
        at = pl.ds(q * PLANE // 4 * SEG, PLANE // 4 * SEG)
        sb3[at, :] = stage3[at, :].astype(BF16)

    @pl.when(mine)
    def _():
        scatter_last(ne, stage3, sb3, rb3, 1 - yh, 0, PLANE - 1, LAST)
        finish(LAST - 1)
        hop_own.wait_recv()
        sum_in[...] = sum_in[...] + sum_own[...]
        all_of(ne, sb3, rb3, 0, PLANE - 1, LAST).wait_send()

    @pl.when(theirs)
    def _():
        scatter_last(ne, stage3, sb3, rb3, yh, 1, 0, LAST + 2)
        finish(LAST - 1)
        kept = e0 * SEG
        for copy in hops:
            copy.wait_recv()
        sum_in[pl.ds(0, kept), :] = sum_in[pl.ds(0, kept), :] + sum_oth[pl.ds(0, kept), :]
        all_of(ne, sb3, rb3, 1, 0, LAST + 2).wait()
        all_of(ne, sb3, rb3, 0, PLANE - 1, LAST).wait_recv()
        add_up(ne, sb3, core * CHIPS + chip, rb3, 2 * PLANE - 1, sum_in, e0)

    value = sum_in[...]
    stage3[pl.ds(0, 8 * SEG), :] = jnp.where(mask[...] > 0.5, value * value, jnp.zeros_like(value))
    for t in range(SEG):
        out[:, t * 128:t * 128 + 128] = stage3[pl.ds(t, 8, stride=SEG), :]

    for copy in y_copies:
        copy.wait_send()

    @pl.when((b < last) & (b != low))
    def _():
        next_copy.wait_send()

    @pl.when((b > 0) & (b != high))
    def _():
        prev_copy.wait_send()

    @pl.when(at_low)
    def _():
        for copy in up_first:
            copy.wait_send()

    @pl.when(at_high)
    def _():
        for copy in down_first:
            copy.wait_send()

    for j in (1, 2, 3):
        @pl.when(b == high + RELAY * j)
        def _():
            up_second[j - 1].wait_send()
    for j in (0, 1, 2):
        @pl.when(b == RELAY * j)
        def _():
            down_second[j].wait_send()

    @pl.when(mine)
    def _():
        for copy in hops:
            copy.wait_send()

    @pl.when(theirs)
    def _():
        hop_own.wait_send()


def on_device(bra, dipole, block_cols, ket, j_upper, sym_upper, j_lower, sym_lower):
    rows, upper = bra.shape
    half = ket.shape[1]
    nbr = rows // BLK
    hbm = pl.BlockSpec(memory_space=pl.ANY)
    dma = lambda n: pltpu.SemaphoreType.DMA((n,))
    box = lambda slots, ne: pltpu.VMEM((slots * ne * SEG, 128), BF16)
    boxes = []
    for ne in (8,) + tuple(ne for _, ne in CHUNKS[:LAST]):
        boxes += [box(CHIPS, ne), box(CHIPS - 1, ne)]
    boxes += [box(PLANE, CHUNKS[LAST][1]), box(2 * PLANE - 1, CHUNKS[LAST][1])]
    sums = pltpu.VMEM((8 * SEG, 128), F32)
    accs = [pltpu.VMEM((upper // NT, ne * PLANE, NT), F32) for ne in (8,) + tuple(ne for _, ne in CHUNKS)]
    sizes = (8,) + tuple(ne for _, ne in CHUNKS)
    stages = [pltpu.VMEM((PLANE * ne * SEG, 128), F32) for ne in sizes]
    pairs = [pltpu.VMEM((CHIPS * ne * SEG, 128), F32) for ne in sizes[:-1]]
    whole = pltpu.SMEM(j_lower.shape, jnp.int32)
    segments = pltpu.VMEM((upper // 128, 128), jnp.int32)
    flops = 2 * rows * 8 * BLK * half + 2 * rows * 2 * half * upper
    return pl.pallas_call(
        kernel,
        out_shape=jax.ShapeDtypeStruct((8, upper), F32),
        in_specs=[hbm] * 8,
        out_specs=pl.BlockSpec(memory_space=pltpu.VMEM),
        scratch_shapes=[
            pltpu.SMEM(block_cols.shape[::-1], jnp.int32), whole, whole, segments, segments,
            pltpu.VMEM((upper // NT, rows, NT), BF16),
            pltpu.VMEM(dipole.shape, BF16),
            pltpu.VMEM((nbr, BLK, half), BF16),
            pltpu.VMEM((nbr + 2 * REACH, BLK, half), BF16),
            pltpu.VMEM((REACH // 4, BLK, half), BF16),
            pltpu.VMEM((half, half), BF16),
            pltpu.VMEM((half, rows), BF16),
            pltpu.VMEM((half, rows), BF16),
            sums,
            *accs,
            *stages,
            *pairs,
            *boxes,
            sums, sums, sums,
            dma(5), dma(upper // NT), dma(len(STEPS)), dma(2), dma(2), dma(2), dma(4), dma(4),
            dma(len(PIECES)), dma(len(PIECES)), dma(LAST + 2), dma(LAST + 2), dma(LAST + 3), dma(LAST + 3), dma(LAST + 2), dma(LAST + 2),
            pltpu.SemaphoreType.REGULAR((2,)),
        ],
        compiler_params=pltpu.CompilerParams(
            collective_id=0, has_side_effects=True, vmem_limit_bytes=56 * 1024 * 1024
        ),
        cost_estimate=pl.CostEstimate(flops=flops, bytes_accessed=28 * 1024 * 1024, transcendentals=0),
    )(
        block_cols.T, j_lower, sym_lower,
        j_upper.reshape(upper // 128, 128), sym_upper.reshape(upper // 128, 128),
        bra, dipole, ket.reshape(nbr, BLK, half),
    )


def solution(mesh):
    return jax.shard_map(
        on_device,
        mesh=mesh,
        in_specs=(
            P("basis", "grp"),
            P("basis", None, None, None),
            P("basis", None),
            P("basis", "grp"),
            P("grp"),
            P("grp"),
            P(),
            P(),
        ),
        out_specs=P("basis", "grp"),
        check_vma=False,
    )
```

```python
import jax
import jax.numpy as jnp
from jax import lax
from jax.experimental import pallas as pl
from jax.experimental.pallas import tpu as pltpu
from jax.sharding import PartitionSpec as P

MESH = pl.DeviceIdType.MESH
F32 = jnp.float32
BF16 = jnp.bfloat16

REACH = 8
BLK = 128
PLANE = 32
LINE = 8
SEG = 16
NT = 512

CHIPS = PLANE // 2
SHIFTS = sorted(
    ((dx, dz) for dz in range(4) for dx in range(4) if dx or dz),
    key=lambda t: -min(t[0], 4 - t[0]) - min(t[1], 4 - t[1]),
)
PLACES = [(dx, dz, dc) for dx, dz in SHIFTS + [(0, 0)] for dc in (1, 0)]
CHUNKS = ((0, 4), (4, 2), (6, 1), (7, 1))
LAST = len(CHUNKS) - 1
PIECES = (
    (0, 8, 2), (0, 10, 6), (0, 16, 4), (0, 20, 4), (1, 8, 16),
    (0, 0, 8), (0, 24, 8), (1, 0, 8), (1, 24, 8),
    (2, 8, 16), (2, 0, 8), (2, 24, 8),
    (3, 8, 16), (3, 0, 8), (3, 24, 6), (3, 30, 2),
)
ARRIVALS = (
    (0, 8, 16), (1, 8, 16), (0, 0, 8), (0, 24, 8), (1, 0, 8), (1, 24, 8),
    (2, 8, 16), (2, 0, 8), (2, 24, 8), (3, 8, 16), (3, 0, 8), (3, 24, 6), (3, 30, 2),
)
INNER = ((8, 2, (0,)), (10, 6, (1,)), (16, 4, (2,)), (20, 4, (3, 4)))
OUTER = ((0, 4, ()), (4, 4, (5,)), (24, 4, ()), (28, 4, (6, 7, 8, 9, 10, 11, 12, 13, 14, 15)))
STEPS = INNER + OUTER
RELAY = 10


def kernel(
    cols_hbm, jl_hbm, sl_hbm, ju_hbm, su_hbm, bra_hbm, dip_hbm, ket_hbm, out,
    cols, jl, sl, ju, su,
    bra, dip, ket_own, ket_ext, relay, perm, app_own, app_oth, mask,
    acc_own, acc0, acc1, acc2, acc3,
    stage_own, stage0, stage1, stage2, stage3, pair_own, pair0, pair1, pair2,
    sb_own, rb_own, sb0, rb0, sb1, rb1, sb2, rb2, sb3, rb3,
    sum_own, sum_oth, sum_in,
    small_sem, bra_sem, dip_sem, ket_sem, halo_send, halo_recv, corner_send, corner_recv,
    y_send, y_recv, pair_send, pair_recv, a_send, a_recv, s_send, s_recv, round_sem,
):
    b = lax.axis_index("basis")
    g = lax.axis_index("grp")
    yh = b // PLANE
    me = b % PLANE
    nbr = dip_hbm.shape[0]
    last = 2 * PLANE - 1
    low, high = PLANE - 1, PLANE
    mine = yh == g
    theirs = yh != g
    across = ((1 - yh) * PLANE + me, g)
    partner = (b, 1 - g)

    def tell(sem, device):
        pl.semaphore_signal(sem, inc=1, device_id=device, device_id_type=MESH)

    barrier = pltpu.get_barrier_semaphore()
    tell(barrier, partner)
    tell(barrier, across)
    for s in range(1, LINE):
        tell(barrier, (yh * PLANE + (me ^ s), g))
    for s in range(1, PLANE // LINE):
        tell(barrier, (yh * PLANE + (me ^ (s * LINE)), g))

    small = [
        pltpu.make_async_copy(src, dst, small_sem.at[i])
        for i, (src, dst) in enumerate(((cols_hbm, cols), (jl_hbm, jl), (sl_hbm, sl), (ju_hbm, ju), (su_hbm, su)))
    ]
    ket_copies = [
        pltpu.make_async_copy(ket_hbm, ket_own, ket_sem.at[0]),
        pltpu.make_async_copy(ket_hbm, ket_ext.at[pl.ds(REACH, nbr)], ket_sem.at[1]),
    ]
    dip_copies = {}
    for i, (r0, n, _) in enumerate(STEPS):
        rows = pl.ds(r0, n)
        dip_copies[r0] = pltpu.make_async_copy(dip_hbm.at[rows], dip.at[rows], dip_sem.at[i])
    bra_copies = [
        pltpu.make_async_copy(bra_hbm.at[:, pl.ds(n * NT, NT)], bra.at[n], bra_sem.at[n])
        for n in range(bra.shape[0])
    ]
    small[0].start()
    dip_copies[STEPS[0][0]].start()
    ket_copies[0].start()
    for r0, _, _ in STEPS[1:4]:
        dip_copies[r0].start()
    ket_copies[1].start()
    for r0, _, _ in STEPS[4:]:
        dip_copies[r0].start()
    @pl.when(me > 0)
    def _():
        tell(barrier, (b - 1, g))

    @pl.when(me < low)
    def _():
        tell(barrier, (b + 1, g))

    at_low, at_high = b == low, b == high
    relays_up = [high + RELAY * j for j in (1, 2, 3)]
    relays_down = [RELAY * j for j in (0, 1, 2)]
    is_up = (b == relays_up[0]) | (b == relays_up[1]) | (b == relays_up[2])
    is_down = (b == relays_down[0]) | (b == relays_down[1]) | (b == relays_down[2])

    @pl.when(at_low)
    def _():
        for peer in [high] + relays_up + relays_down:
            tell(barrier, (peer, g))

    @pl.when(at_high)
    def _():
        for peer in [low] + relays_up + relays_down:
            tell(barrier, (peer, g))

    @pl.when(is_up | is_down)
    def _():
        tell(barrier, (low, g))
        tell(barrier, (high, g))

    size = perm.shape[0]
    place = lax.broadcasted_iota(jnp.int32, (size, size), 0)
    state = lax.broadcasted_iota(jnp.int32, (size, size), 1)
    region = place & (PLANE - 1)
    wanted = (2 * (region & (CHIPS - 1)) + region // CHIPS) * 8 + place // PLANE
    perm[...] = jnp.where(state == wanted, 1.0, 0.0).astype(BF16)

    def apply_rows(r0, n, ket, base):
        def one(i, carry):
            r = r0 + i
            top = ket.shape[0] - 1
            blocks = [ket[jnp.clip(cols[k, r] - base, 0, top)] for k in range(cols.shape[0])]
            row = jnp.concatenate([dip[r, k] for k in range(cols.shape[0])], axis=1)
            value = jnp.dot(row, jnp.concatenate(blocks, axis=0), preferred_element_type=F32)
            turned = lax.dot_general(
                perm[...], value.astype(BF16), (((1,), (1,)), ((), ())), preferred_element_type=F32
            )
            app_own[:, pl.ds(pl.multiple_of(r * BLK, BLK), BLK)] = turned.astype(BF16)
            return carry

        lax.fori_loop(0, n, one, 0)

    def to_next(dst):
        return pltpu.make_async_remote_copy(
            ket_hbm.at[pl.ds(nbr - REACH, REACH)], ket_ext.at[pl.ds(0, REACH)],
            halo_send.at[0], halo_recv.at[0], device_id=(dst, g), device_id_type=MESH,
        )

    def to_prev(dst):
        return pltpu.make_async_remote_copy(
            ket_hbm.at[pl.ds(0, REACH)], ket_ext.at[pl.ds(REACH + nbr, REACH)],
            halo_send.at[1], halo_recv.at[1], device_id=(dst, g), device_id_type=MESH,
        )

    next_copy, prev_copy = to_next(jnp.minimum(b + 1, last)), to_prev(jnp.maximum(b - 1, 0))
    quarter = REACH // 4

    def corner(src, dst, sem, device):
        return pltpu.make_async_remote_copy(
            src, dst, corner_send.at[sem], corner_recv.at[sem], device_id=(device, g), device_id_type=MESH
        )

    def ket_part(start, j):
        return ket_hbm.at[pl.ds(start + quarter * j, quarter)]

    def ext_part(start, j):
        return ket_ext.at[pl.ds(start + quarter * j, quarter)]

    up_first = [corner(ket_part(nbr - REACH, 0), ext_part(0, 0), 0, high)]
    up_first += [corner(ket_part(nbr - REACH, j), relay, j, high + RELAY * j) for j in (1, 2, 3)]
    up_second = [corner(relay, ext_part(0, j), j, high) for j in (1, 2, 3)]
    down_first = [corner(ket_part(0, 3), ext_part(REACH + nbr, 3), 3, low)]
    down_first += [corner(ket_part(0, j), relay, j, RELAY * j) for j in (0, 1, 2)]
    down_second = [corner(relay, ext_part(REACH + nbr, j), j, low) for j in (0, 1, 2)]

    def relay_on():
        for j in (1, 2, 3):
            @pl.when(b == high + RELAY * j)
            def _():
                up_first[j].wait_recv()
                up_second[j - 1].start()
        for j in (0, 1, 2):
            @pl.when(b == RELAY * j)
            def _():
                down_first[j + 1].wait_recv()
                down_second[j].start()

    def halo_wait():
        ket_copies[1].wait()

        @pl.when((b > 0) & (b != high))
        def _():
            next_copy.wait_recv()

        @pl.when((b < last) & (b != low))
        def _():
            prev_copy.wait_recv()

        @pl.when(at_high)
        def _():
            up_first[0].wait_recv()
            for copy in up_second:
                copy.wait_recv()

        @pl.when(at_low)
        def _():
            down_first[0].wait_recv()
            for copy in down_second:
                copy.wait_recv()

    y_copies = []
    for i, (c, r0, n) in enumerate(PIECES):
        e0, ne = CHUNKS[c]
        part = (pl.ds(e0 * PLANE, ne * PLANE), pl.ds(r0 * BLK, n * BLK))
        y_copies.append(
            pltpu.make_async_remote_copy(
                app_own.at[part], app_oth.at[part], y_send.at[i], y_recv.at[i],
                device_id=partner, device_id_type=MESH,
            )
        )

    def enter():
        many = jnp.where(at_low | at_high, 7, jnp.where(is_up | is_down, 2, 0))
        ends = jnp.where(me > 0, 1, 0) + jnp.where(me < low, 1, 0)
        pl.semaphore_wait(barrier, LINE + PLANE // LINE + ends + many)

        @pl.when((b < last) & (b != low))
        def _():
            next_copy.start()

        @pl.when((b > 0) & (b != high))
        def _():
            prev_copy.start()

        @pl.when(at_low)
        def _():
            for copy in up_first:
                copy.start()

        @pl.when(at_high)
        def _():
            for copy in down_first:
                copy.start()

    def apply_step(r0, n, ready, ket, base):
        dip_copies[r0].wait()
        apply_rows(r0, n, ket, base)
        if r0 == INNER[0][0]:
            enter()
        for k in ready:
            y_copies[k].start()

    def spread(value, stage, ne, first):
        for h in range(value.shape[1] // 128):
            for q in range(value.shape[0] // 8):
                e, o = q // (PLANE // 8), (q % (PLANE // 8)) * 8
                at = pl.ds(o * SEG * ne + e * SEG + first + h, 8, stride=SEG * ne)
                stage[at, :] = value[q * 8:q * 8 + 8, h * 128:h * 128 + 128]

    def contract(lhs, acc, stage, e0, ne, r0, n, begin, end):
        k = pl.ds(r0 * BLK, n * BLK)

        def one(t, carry):
            value = jnp.dot(
                lhs[pl.ds(e0 * PLANE, ne * PLANE), k], bra[t, k, :], preferred_element_type=F32
            )
            if not begin:
                value = value + acc[t]
            if end:
                spread(value, stage, ne, t * (NT // 128))
            else:
                acc[t] = value
            return carry

        if ne > 2:
            lax.fori_loop(0, bra.shape[0], one, 0)
        else:
            for t in range(bra.shape[0]):
                one(t, 0)

    core = me & 1
    chip = me // 2

    def meet(ne, stage, pair, sem):
        rows = CHIPS * ne * SEG
        theirs_at = pl.ds(pl.multiple_of((1 - core) * rows, rows), rows)
        return pltpu.make_async_remote_copy(
            stage.at[theirs_at], pair, pair_send.at[sem], pair_recv.at[sem],
            device_id=(b ^ 1, g), device_id_type=MESH,
        )

    def scatter(ne, stage, pair, sb, rb, sem):
        rows = ne * SEG
        meet(ne, stage, pair, sem).wait()

        def one(o, carry):
            at = pl.ds(pl.multiple_of(o * 4 * rows, 4 * rows), 4 * rows)
            own = pl.ds(pl.multiple_of(core * CHIPS * rows + o * 4 * rows, 4 * rows), 4 * rows)
            sb[at, :] = (stage[own, :] + pair[at, :]).astype(BF16)
            return carry

        lax.fori_loop(0, CHIPS // 4, one, 0)
        for slot, (dx, dz) in enumerate(SHIFTS):
            owner = (chip // 4 + dz) % 4 * 4 + (chip % 4 + dx) % 4
            pltpu.make_async_remote_copy(
                sb.at[pl.ds(pl.multiple_of(owner * rows, rows), rows)], rb.at[pl.ds(slot * rows, rows)],
                a_send.at[sem], a_recv.at[sem],
                device_id=(yh * PLANE + 2 * owner + core, g), device_id_type=MESH,
            ).start()

    def take(ne, sb, rb, sem, total, e0):
        rows = ne * SEG
        pltpu.make_async_remote_copy(
            sb.at[pl.ds(0, (CHIPS - 1) * rows)], rb, a_send.at[sem], a_recv.at[sem],
            device_id=partner, device_id_type=MESH,
        ).wait()
        add_up(ne, sb, chip, rb, CHIPS - 1, total, e0)

    def add_up(ne, sb, region, rb, slots, total, e0):
        rows = ne * SEG

        def one(s, value):
            return value + rb[pl.ds(pl.multiple_of(s * rows, rows), rows), :].astype(F32)

        value = sb[pl.ds(pl.multiple_of(region * rows, rows), rows), :].astype(F32)
        total[pl.ds(e0 * SEG, rows), :] = lax.fori_loop(0, slots, one, value)

    def scatter_last(ne, sb, rb, plane, count, slot, sem):
        rows = ne * SEG
        for s, (dx, dz, dc) in enumerate(PLACES[:count]):
            to_chip = (chip // 4 + dz) % 4 * 4 + (chip % 4 + dx) % 4
            to_core = core ^ dc
            region = to_core * CHIPS + to_chip
            pltpu.make_async_remote_copy(
                sb.at[pl.ds(pl.multiple_of(region * rows, rows), rows)], rb.at[pl.ds((slot + s) * rows, rows)],
                a_send.at[sem], a_recv.at[sem],
                device_id=(plane * PLANE + 2 * to_chip + to_core, g), device_id_type=MESH,
            ).start()

    def all_of(ne, sb, rb, begin, slot, sem):
        rows = ne * SEG
        return pltpu.make_async_remote_copy(
            sb.at[pl.ds(0, (PLANE - begin) * rows)], rb.at[pl.ds(slot * rows, (PLANE - begin) * rows)],
            a_send.at[sem], a_recv.at[sem], device_id=partner, device_id_type=MESH,
        )

    def hop(total, e0, ne, sem):
        part = pl.ds(e0 * SEG, ne * SEG)
        return pltpu.make_async_remote_copy(
            total.at[part], sum_in.at[part], s_send.at[sem], s_recv.at[sem],
            device_id=across, device_id_type=MESH,
        )

    OWN = LAST + 1
    hop_own = hop(sum_own, 0, 8, OWN)
    hops = [hop(sum_oth, e0, ne, c) for c, (e0, ne) in enumerate(CHUNKS[:LAST])]
    boxes = ((sb0, rb0), (sb1, rb1), (sb2, rb2))
    stages = (stage0, stage1, stage2, stage3)
    pairs = (pair0, pair1, pair2)

    def finish(c):
        e0, ne = CHUNKS[c]
        take(ne, *boxes[c], c, sum_oth, e0)

        @pl.when(mine)
        def _():
            hops[c].start()

    def main():
        small[0].wait()
        ket_copies[0].wait()
        for r0, n, ready in INNER:
            apply_step(r0, n, ready, ket_own, b * nbr)
            if r0 == INNER[0][0]:
                for copy in bra_copies:
                    copy.start()
                for copy in small[1:]:
                    copy.start()
            if r0 == INNER[1][0]:
                for s in range(1, PLANE // LINE):
                    tell(round_sem.at[0], (yh * PLANE + (me ^ (s * LINE)), g))
        relay_on()
        for copy in bra_copies:
            copy.wait()
        contract(app_own, acc_own, stage_own, 0, 8, REACH, nbr - 2 * REACH, True, False)
        pl.semaphore_wait(round_sem.at[0], PLANE // LINE - 1)
        tell(round_sem.at[1], across)
        halo_wait()
        for r0, n, ready in OUTER:
            apply_step(r0, n, ready, ket_ext, b * nbr - REACH)
        contract(app_own, acc_own, stage_own, 0, 8, 0, REACH, False, False)
        contract(app_own, acc_own, stage_own, 0, 8, nbr - REACH, REACH, False, True)
        meet(8, stage_own, pair_own, OWN).start()
        pl.semaphore_wait(round_sem.at[1], 1)

    main()

    def rules():
        for copy in small[1:]:
            copy.wait()
        for e in range(8):
            allowed = (jnp.abs(jl[8 * b + e] - ju[...]) <= 1) & (su[...] != sl[8 * b + e])
            mask[pl.ds(e * SEG, SEG), :] = jnp.where(allowed, 1.0, 0.0)

    def finish_own():
        take(8, sb_own, rb_own, OWN, sum_own, 0)

        @pl.when(theirs)
        def _():
            hop_own.start()

    accs = (acc0, acc1, acc2, acc3)
    seen = [0] * len(CHUNKS)
    for i, (c, r0, n) in enumerate(ARRIVALS):
        e0, ne = CHUNKS[c]
        for copy, (cc, p0, m) in zip(y_copies, PIECES):
            if cc == c and r0 <= p0 and p0 + m <= r0 + n:
                copy.wait_recv()
        full = seen[c] + n == nbr
        contract(app_oth, accs[c], stages[c], e0, ne, r0, n, seen[c] == 0, full)
        seen[c] += n
        if full and c < LAST:
            meet(ne, stages[c], pairs[c], c).start()
        if i == 0:
            scatter(8, stage_own, pair_own, sb_own, rb_own, OWN)
        if i == 3:
            finish_own()
        if i == 5:
            rules()
        if full and c < LAST:
            scatter(ne, stages[c], pairs[c], *boxes[c], c)
        if i == 6:
            finish(0)
    e0, ne = CHUNKS[LAST]
    for q in range(4):
        at = pl.ds(q * PLANE // 4 * SEG, PLANE // 4 * SEG)
        sb3[at, :] = stage3[at, :].astype(BF16)

    @pl.when(mine)
    def _():
        scatter_last(ne, sb3, rb3, 1 - yh, PLANE, PLANE - 1, LAST)
        finish(LAST - 2)
        finish(LAST - 1)
        hop_own.wait_recv()
        sum_in[...] = sum_in[...] + sum_own[...]
        all_of(ne, sb3, rb3, 0, PLANE - 1, LAST).wait_send()

    @pl.when(theirs)
    def _():
        scatter_last(ne, sb3, rb3, yh, PLANE - 1, 0, LAST + 2)
        finish(LAST - 2)
        finish(LAST - 1)
        kept = e0 * SEG
        for copy in hops:
            copy.wait_recv()
        sum_in[pl.ds(0, kept), :] = sum_in[pl.ds(0, kept), :] + sum_oth[pl.ds(0, kept), :]
        rows = ne * SEG
        region = core * CHIPS + chip
        value = sb3[pl.ds(pl.multiple_of(region * rows, rows), rows), :].astype(F32)
        all_of(ne, sb3, rb3, 1, 0, LAST + 2).wait()
        for s in range(PLANE - 1):
            value = value + rb3[pl.ds(s * rows, rows), :].astype(F32)
        all_of(ne, sb3, rb3, 0, PLANE - 1, LAST).wait_recv()
        for s in range(PLANE - 1, 2 * PLANE - 1):
            value = value + rb3[pl.ds(s * rows, rows), :].astype(F32)
        sum_in[pl.ds(e0 * SEG, rows), :] = value

    value = sum_in[...]
    stage3[pl.ds(0, 8 * SEG), :] = jnp.where(mask[...] > 0.5, value * value, jnp.zeros_like(value))
    for t in range(SEG):
        out[:, t * 128:t * 128 + 128] = stage3[pl.ds(t, 8, stride=SEG), :]

    for copy in y_copies:
        copy.wait_send()

    @pl.when((b < last) & (b != low))
    def _():
        next_copy.wait_send()

    @pl.when((b > 0) & (b != high))
    def _():
        prev_copy.wait_send()

    @pl.when(at_low)
    def _():
        for copy in up_first:
            copy.wait_send()

    @pl.when(at_high)
    def _():
        for copy in down_first:
            copy.wait_send()

    for j in (1, 2, 3):
        @pl.when(b == high + RELAY * j)
        def _():
            up_second[j - 1].wait_send()
    for j in (0, 1, 2):
        @pl.when(b == RELAY * j)
        def _():
            down_second[j].wait_send()

    @pl.when(mine)
    def _():
        for copy in hops:
            copy.wait_send()

    @pl.when(theirs)
    def _():
        hop_own.wait_send()


def on_device(bra, dipole, block_cols, ket, j_upper, sym_upper, j_lower, sym_lower):
    rows, upper = bra.shape
    half = ket.shape[1]
    nbr = rows // BLK
    hbm = pl.BlockSpec(memory_space=pl.ANY)
    dma = lambda n: pltpu.SemaphoreType.DMA((n,))
    box = lambda slots, ne: pltpu.VMEM((slots * ne * SEG, 128), BF16)
    boxes = []
    for ne in (8,) + tuple(ne for _, ne in CHUNKS[:LAST]):
        boxes += [box(CHIPS, ne), box(CHIPS - 1, ne)]
    boxes += [box(PLANE, CHUNKS[LAST][1]), box(2 * PLANE - 1, CHUNKS[LAST][1])]
    sums = pltpu.VMEM((8 * SEG, 128), F32)
    accs = [pltpu.VMEM((upper // NT, ne * PLANE, NT), F32) for ne in (8,) + tuple(ne for _, ne in CHUNKS)]
    sizes = (8,) + tuple(ne for _, ne in CHUNKS)
    stages = [pltpu.VMEM((PLANE * ne * SEG, 128), F32) for ne in sizes]
    pairs = [pltpu.VMEM((CHIPS * ne * SEG, 128), F32) for ne in sizes[:-1]]
    whole = pltpu.SMEM(j_lower.shape, jnp.int32)
    segments = pltpu.VMEM((upper // 128, 128), jnp.int32)
    flops = 2 * rows * 8 * BLK * half + 2 * rows * 2 * half * upper
    return pl.pallas_call(
        kernel,
        out_shape=jax.ShapeDtypeStruct((8, upper), F32),
        in_specs=[hbm] * 8,
        out_specs=pl.BlockSpec(memory_space=pltpu.VMEM),
        scratch_shapes=[
            pltpu.SMEM(block_cols.shape[::-1], jnp.int32), whole, whole, segments, segments,
            pltpu.VMEM((upper // NT, rows, NT), BF16),
            pltpu.VMEM(dipole.shape, BF16),
            pltpu.VMEM((nbr, BLK, half), BF16),
            pltpu.VMEM((nbr + 2 * REACH, BLK, half), BF16),
            pltpu.VMEM((REACH // 4, BLK, half), BF16),
            pltpu.VMEM((half, half), BF16),
            pltpu.VMEM((half, rows), BF16),
            pltpu.VMEM((half, rows), BF16),
            sums,
            *accs,
            *stages,
            *pairs,
            *boxes,
            sums, sums, sums,
            dma(5), dma(upper // NT), dma(len(STEPS)), dma(2), dma(2), dma(2), dma(4), dma(4),
            dma(len(PIECES)), dma(len(PIECES)), dma(LAST + 2), dma(LAST + 2), dma(LAST + 3), dma(LAST + 3), dma(LAST + 2), dma(LAST + 2),
            pltpu.SemaphoreType.REGULAR((2,)),
        ],
        compiler_params=pltpu.CompilerParams(
            collective_id=0, has_side_effects=True, vmem_limit_bytes=56 * 1024 * 1024
        ),
        cost_estimate=pl.CostEstimate(flops=flops, bytes_accessed=28 * 1024 * 1024, transcendentals=0),
    )(
        block_cols.T, j_lower, sym_lower,
        j_upper.reshape(upper // 128, 128), sym_upper.reshape(upper // 128, 128),
        bra, dipole, ket.reshape(nbr, BLK, half),
    )


def solution(mesh):
    return jax.shard_map(
        on_device,
        mesh=mesh,
        in_specs=(
            P("basis", "grp"),
            P("basis", None, None, None),
            P("basis", None),
            P("basis", "grp"),
            P("grp"),
            P("grp"),
            P(),
            P(),
        ),
        out_specs=P("basis", "grp"),
        check_vma=False,
    )
```

```python
import jax
import jax.numpy as jnp
from jax import lax
from jax.experimental import pallas as pl
from jax.experimental.pallas import tpu as pltpu
from jax.sharding import PartitionSpec as P

MESH = pl.DeviceIdType.MESH
F32 = jnp.float32
BF16 = jnp.bfloat16

REACH = 8
BLK = 128
PLANE = 32
LINE = 8
SEG = 16
NT = 512

CHIPS = PLANE // 2
SHIFTS = sorted(
    ((dx, dz) for dz in range(4) for dx in range(4) if dx or dz),
    key=lambda t: -min(t[0], 4 - t[0]) - min(t[1], 4 - t[1]),
)
PLACES = [(dx, dz, dc) for dx, dz in SHIFTS + [(0, 0)] for dc in (1, 0)]
CHUNKS = ((0, 4), (4, 2), (6, 1), (7, 1))
LAST = len(CHUNKS) - 1
PIECES = (
    (0, 8, 1), (0, 9, 3), (0, 12, 4), (0, 16, 4), (0, 20, 4), (1, 8, 16),
    (0, 0, 8), (0, 24, 8), (1, 0, 8), (1, 24, 8),
    (2, 8, 16), (2, 0, 8), (2, 24, 8),
    (3, 8, 16), (3, 0, 8), (3, 24, 6), (3, 30, 2),
)
ARRIVALS = (
    (0, 8, 16), (1, 8, 16), (0, 0, 8), (0, 24, 8), (1, 0, 8), (1, 24, 8),
    (2, 8, 16), (2, 0, 8), (2, 24, 8), (3, 8, 16), (3, 0, 8), (3, 24, 6), (3, 30, 2),
)
INNER = ((8, 1, (0,)), (9, 3, (1,)), (12, 4, (2,)), (16, 4, (3,)), (20, 4, (4, 5)))
OUTER = ((0, 4, ()), (4, 4, (6,)), (24, 4, ()), (28, 4, (7, 8, 9, 10, 11, 12, 13, 14, 15, 16)))
STEPS = INNER + OUTER
UP = 24


def kernel(
    cols_hbm, jl_hbm, sl_hbm, ju_hbm, su_hbm, bra_hbm, dip_hbm, ket_hbm, out,
    cols, jl, sl, ju, su,
    bra, dip, ket_own, ket_ext, relay, perm, app_own, app_oth, mask,
    acc_own, acc0, acc1, acc2, acc3,
    stage_own, stage0, stage1, stage2, stage3, pair_own, pair0, pair1, pair2,
    sb_own, rb_own, sb0, rb0, sb1, rb1, sb2, rb2, sb3, rb3,
    sum_own, sum_oth, sum_in,
    small_sem, bra_sem, dip_sem, ket_sem, halo_send, halo_recv, corner_send, corner_recv,
    y_send, y_recv, pair_send, pair_recv, a_send, a_recv, s_send, s_recv, round_sem,
):
    b = lax.axis_index("basis")
    g = lax.axis_index("grp")
    yh = b // PLANE
    me = b % PLANE
    nbr = dip_hbm.shape[0]
    last = 2 * PLANE - 1
    low, high = PLANE - 1, PLANE
    mine = yh == g
    theirs = yh != g
    across = ((1 - yh) * PLANE + me, g)
    partner = (b, 1 - g)

    def tell(sem, device):
        pl.semaphore_signal(sem, inc=1, device_id=device, device_id_type=MESH)

    barrier = pltpu.get_barrier_semaphore()
    tell(barrier, partner)
    tell(barrier, across)
    for s in range(1, LINE):
        tell(barrier, (yh * PLANE + (me ^ s), g))
    for s in range(1, PLANE // LINE):
        tell(barrier, (yh * PLANE + (me ^ (s * LINE)), g))

    small = [
        pltpu.make_async_copy(src, dst, small_sem.at[i])
        for i, (src, dst) in enumerate(((cols_hbm, cols), (jl_hbm, jl), (sl_hbm, sl), (ju_hbm, ju), (su_hbm, su)))
    ]
    ket_copies = [
        pltpu.make_async_copy(ket_hbm, ket_own, ket_sem.at[0]),
        pltpu.make_async_copy(ket_hbm, ket_ext.at[pl.ds(REACH, nbr)], ket_sem.at[1]),
    ]
    dip_copies = {}
    for i, (r0, n, _) in enumerate(STEPS):
        rows = pl.ds(r0, n)
        dip_copies[r0] = pltpu.make_async_copy(dip_hbm.at[rows], dip.at[rows], dip_sem.at[i])
    bra_copies = [
        pltpu.make_async_copy(bra_hbm.at[:, pl.ds(n * NT, NT)], bra.at[n], bra_sem.at[n])
        for n in range(bra.shape[0])
    ]
    small[0].start()
    dip_copies[STEPS[0][0]].start()
    ket_copies[0].start()
    for r0, _, _ in STEPS[1:4]:
        dip_copies[r0].start()
    ket_copies[1].start()
    for r0, _, _ in STEPS[4:]:
        dip_copies[r0].start()
    @pl.when(me > 0)
    def _():
        tell(barrier, (b - 1, g))

    @pl.when(me < low)
    def _():
        tell(barrier, (b + 1, g))

    at_low, at_high = b == low, b == high
    relays_up = [high + UP + 2 * j for j in (1, 2, 3)]
    relays_down = [2 * j for j in (0, 1, 2)]
    is_up = (b == relays_up[0]) | (b == relays_up[1]) | (b == relays_up[2])
    is_down = (b == relays_down[0]) | (b == relays_down[1]) | (b == relays_down[2])

    @pl.when(at_low)
    def _():
        for peer in [high] + relays_up + relays_down:
            tell(barrier, (peer, g))

    @pl.when(at_high)
    def _():
        for peer in [low] + relays_up + relays_down:
            tell(barrier, (peer, g))

    @pl.when(is_up | is_down)
    def _():
        tell(barrier, (low, g))
        tell(barrier, (high, g))

    size = perm.shape[0]
    place = lax.broadcasted_iota(jnp.int32, (size, size), 0)
    state = lax.broadcasted_iota(jnp.int32, (size, size), 1)
    region = place & (PLANE - 1)
    wanted = (2 * (region & (CHIPS - 1)) + region // CHIPS) * 8 + place // PLANE
    perm[...] = jnp.where(state == wanted, 1.0, 0.0).astype(BF16)

    def apply_rows(r0, n, ket, base):
        def one(i, carry):
            r = r0 + i
            top = ket.shape[0] - 1
            blocks = [ket[jnp.clip(cols[k, r] - base, 0, top)] for k in range(cols.shape[0])]
            row = jnp.concatenate([dip[r, k] for k in range(cols.shape[0])], axis=1)
            value = jnp.dot(row, jnp.concatenate(blocks, axis=0), preferred_element_type=F32)
            turned = lax.dot_general(
                perm[...], value.astype(BF16), (((1,), (1,)), ((), ())), preferred_element_type=F32
            )
            app_own[:, pl.ds(pl.multiple_of(r * BLK, BLK), BLK)] = turned.astype(BF16)
            return carry

        lax.fori_loop(0, n, one, 0)

    def to_next(dst):
        return pltpu.make_async_remote_copy(
            ket_hbm.at[pl.ds(nbr - REACH, REACH)], ket_ext.at[pl.ds(0, REACH)],
            halo_send.at[0], halo_recv.at[0], device_id=(dst, g), device_id_type=MESH,
        )

    def to_prev(dst):
        return pltpu.make_async_remote_copy(
            ket_hbm.at[pl.ds(0, REACH)], ket_ext.at[pl.ds(REACH + nbr, REACH)],
            halo_send.at[1], halo_recv.at[1], device_id=(dst, g), device_id_type=MESH,
        )

    next_copy, prev_copy = to_next(jnp.minimum(b + 1, last)), to_prev(jnp.maximum(b - 1, 0))
    quarter = REACH // 4

    def corner(src, dst, sem, device):
        return pltpu.make_async_remote_copy(
            src, dst, corner_send.at[sem], corner_recv.at[sem], device_id=(device, g), device_id_type=MESH
        )

    def ket_part(start, j):
        return ket_hbm.at[pl.ds(start + quarter * j, quarter)]

    def ext_part(start, j):
        return ket_ext.at[pl.ds(start + quarter * j, quarter)]

    up_first = [corner(ket_part(nbr - REACH, 0), ext_part(0, 0), 0, high)]
    up_first += [corner(ket_part(nbr - REACH, j), relay, j, high + UP + 2 * j) for j in (1, 2, 3)]
    up_second = [corner(relay, ext_part(0, j), j, high) for j in (1, 2, 3)]
    down_first = [corner(ket_part(0, 3), ext_part(REACH + nbr, 3), 3, low)]
    down_first += [corner(ket_part(0, j), relay, j, 2 * j) for j in (0, 1, 2)]
    down_second = [corner(relay, ext_part(REACH + nbr, j), j, low) for j in (0, 1, 2)]

    def relay_on():
        for j in (1, 2, 3):
            @pl.when(b == high + UP + 2 * j)
            def _():
                up_first[j].wait_recv()
                up_second[j - 1].start()
        for j in (0, 1, 2):
            @pl.when(b == 2 * j)
            def _():
                down_first[j + 1].wait_recv()
                down_second[j].start()

    def halo_wait():
        ket_copies[1].wait()

        @pl.when((b > 0) & (b != high))
        def _():
            next_copy.wait_recv()

        @pl.when((b < last) & (b != low))
        def _():
            prev_copy.wait_recv()

        @pl.when(at_high)
        def _():
            up_first[0].wait_recv()
            for copy in up_second:
                copy.wait_recv()

        @pl.when(at_low)
        def _():
            down_first[0].wait_recv()
            for copy in down_second:
                copy.wait_recv()

    y_copies = []
    for i, (c, r0, n) in enumerate(PIECES):
        e0, ne = CHUNKS[c]
        part = (pl.ds(e0 * PLANE, ne * PLANE), pl.ds(r0 * BLK, n * BLK))
        y_copies.append(
            pltpu.make_async_remote_copy(
                app_own.at[part], app_oth.at[part], y_send.at[i], y_recv.at[i],
                device_id=partner, device_id_type=MESH,
            )
        )

    def enter():
        many = jnp.where(at_low | at_high, 7, jnp.where(is_up | is_down, 2, 0))
        ends = jnp.where(me > 0, 1, 0) + jnp.where(me < low, 1, 0)
        pl.semaphore_wait(barrier, LINE + PLANE // LINE + ends + many)

        @pl.when((b < last) & (b != low))
        def _():
            next_copy.start()

        @pl.when((b > 0) & (b != high))
        def _():
            prev_copy.start()

        @pl.when(at_low)
        def _():
            for copy in up_first:
                copy.start()

        @pl.when(at_high)
        def _():
            for copy in down_first:
                copy.start()

    def apply_step(r0, n, ready, ket, base):
        dip_copies[r0].wait()
        apply_rows(r0, n, ket, base)
        if r0 == INNER[0][0]:
            enter()
        for k in ready:
            y_copies[k].start()

    def spread(value, stage, ne, first):
        for h in range(value.shape[1] // 128):
            for q in range(value.shape[0] // 8):
                e, o = q // (PLANE // 8), (q % (PLANE // 8)) * 8
                at = pl.ds(o * SEG * ne + e * SEG + first + h, 8, stride=SEG * ne)
                stage[at, :] = value[q * 8:q * 8 + 8, h * 128:h * 128 + 128]

    def contract(lhs, acc, stage, e0, ne, r0, n, begin, end):
        k = pl.ds(r0 * BLK, n * BLK)

        def one(t, carry):
            value = jnp.dot(
                lhs[pl.ds(e0 * PLANE, ne * PLANE), k], bra[t, k, :], preferred_element_type=F32
            )
            if not begin:
                value = value + acc[t]
            if end:
                spread(value, stage, ne, t * (NT // 128))
            else:
                acc[t] = value
            return carry

        if ne > 2:
            lax.fori_loop(0, bra.shape[0], one, 0)
        else:
            for t in range(bra.shape[0]):
                one(t, 0)

    core = me & 1
    chip = me // 2

    def meet(ne, stage, pair, sem):
        rows = CHIPS * ne * SEG
        theirs_at = pl.ds(pl.multiple_of((1 - core) * rows, rows), rows)
        return pltpu.make_async_remote_copy(
            stage.at[theirs_at], pair, pair_send.at[sem], pair_recv.at[sem],
            device_id=(b ^ 1, g), device_id_type=MESH,
        )

    def scatter(ne, stage, pair, sb, rb, sem):
        rows = ne * SEG
        meet(ne, stage, pair, sem).wait()

        def one(o, carry):
            at = pl.ds(pl.multiple_of(o * 4 * rows, 4 * rows), 4 * rows)
            own = pl.ds(pl.multiple_of(core * CHIPS * rows + o * 4 * rows, 4 * rows), 4 * rows)
            sb[at, :] = (stage[own, :] + pair[at, :]).astype(BF16)
            return carry

        lax.fori_loop(0, CHIPS // 4, one, 0)
        for slot, (dx, dz) in enumerate(SHIFTS):
            owner = (chip // 4 + dz) % 4 * 4 + (chip % 4 + dx) % 4
            pltpu.make_async_remote_copy(
                sb.at[pl.ds(pl.multiple_of(owner * rows, rows), rows)], rb.at[pl.ds(slot * rows, rows)],
                a_send.at[sem], a_recv.at[sem],
                device_id=(yh * PLANE + 2 * owner + core, g), device_id_type=MESH,
            ).start()

    def take(ne, sb, rb, sem, total, e0):
        rows = ne * SEG
        pltpu.make_async_remote_copy(
            sb.at[pl.ds(0, (CHIPS - 1) * rows)], rb, a_send.at[sem], a_recv.at[sem],
            device_id=partner, device_id_type=MESH,
        ).wait()
        add_up(ne, sb, chip, rb, CHIPS - 1, total, e0)

    def add_up(ne, sb, region, rb, slots, total, e0):
        rows = ne * SEG

        def one(s, value):
            return value + rb[pl.ds(pl.multiple_of(s * rows, rows), rows), :].astype(F32)

        value = sb[pl.ds(pl.multiple_of(region * rows, rows), rows), :].astype(F32)
        total[pl.ds(e0 * SEG, rows), :] = lax.fori_loop(0, slots, one, value)

    def scatter_last(ne, sb, rb, plane, count, slot, sem):
        rows = ne * SEG
        for s, (dx, dz, dc) in enumerate(PLACES[:count]):
            to_chip = (chip // 4 + dz) % 4 * 4 + (chip % 4 + dx) % 4
            to_core = core ^ dc
            region = to_core * CHIPS + to_chip
            pltpu.make_async_remote_copy(
                sb.at[pl.ds(pl.multiple_of(region * rows, rows), rows)], rb.at[pl.ds((slot + s) * rows, rows)],
                a_send.at[sem], a_recv.at[sem],
                device_id=(plane * PLANE + 2 * to_chip + to_core, g), device_id_type=MESH,
            ).start()

    def all_of(ne, sb, rb, begin, slot, sem):
        rows = ne * SEG
        return pltpu.make_async_remote_copy(
            sb.at[pl.ds(0, (PLANE - begin) * rows)], rb.at[pl.ds(slot * rows, (PLANE - begin) * rows)],
            a_send.at[sem], a_recv.at[sem], device_id=partner, device_id_type=MESH,
        )

    def hop(total, e0, ne, sem):
        part = pl.ds(e0 * SEG, ne * SEG)
        return pltpu.make_async_remote_copy(
            total.at[part], sum_in.at[part], s_send.at[sem], s_recv.at[sem],
            device_id=across, device_id_type=MESH,
        )

    OWN = LAST + 1
    hop_own = hop(sum_own, 0, 8, OWN)
    hops = [hop(sum_oth, e0, ne, c) for c, (e0, ne) in enumerate(CHUNKS[:LAST])]
    boxes = ((sb0, rb0), (sb1, rb1), (sb2, rb2))
    stages = (stage0, stage1, stage2, stage3)
    pairs = (pair0, pair1, pair2)

    def finish(c):
        e0, ne = CHUNKS[c]
        take(ne, *boxes[c], c, sum_oth, e0)

        @pl.when(mine)
        def _():
            hops[c].start()

    def main():
        small[0].wait()
        ket_copies[0].wait()
        for r0, n, ready in INNER:
            apply_step(r0, n, ready, ket_own, b * nbr)
            if r0 == INNER[0][0]:
                for copy in bra_copies:
                    copy.start()
                for copy in small[1:]:
                    copy.start()
            if r0 == INNER[1][0]:
                for s in range(1, PLANE // LINE):
                    tell(round_sem.at[0], (yh * PLANE + (me ^ (s * LINE)), g))
        relay_on()
        for copy in bra_copies:
            copy.wait()
        contract(app_own, acc_own, stage_own, 0, 8, REACH, nbr - 2 * REACH, True, False)
        pl.semaphore_wait(round_sem.at[0], PLANE // LINE - 1)
        tell(round_sem.at[1], across)
        halo_wait()
        for r0, n, ready in OUTER:
            apply_step(r0, n, ready, ket_ext, b * nbr - REACH)
        contract(app_own, acc_own, stage_own, 0, 8, 0, REACH, False, False)
        contract(app_own, acc_own, stage_own, 0, 8, nbr - REACH, REACH, False, True)
        meet(8, stage_own, pair_own, OWN).start()
        pl.semaphore_wait(round_sem.at[1], 1)

    main()

    def rules():
        for copy in small[1:]:
            copy.wait()
        for e in range(8):
            allowed = (jnp.abs(jl[8 * b + e] - ju[...]) <= 1) & (su[...] != sl[8 * b + e])
            mask[pl.ds(e * SEG, SEG), :] = jnp.where(allowed, 1.0, 0.0)

    def finish_own():
        take(8, sb_own, rb_own, OWN, sum_own, 0)

        @pl.when(theirs)
        def _():
            hop_own.start()

    accs = (acc0, acc1, acc2, acc3)
    seen = [0] * len(CHUNKS)
    for i, (c, r0, n) in enumerate(ARRIVALS):
        e0, ne = CHUNKS[c]
        for copy, (cc, p0, m) in zip(y_copies, PIECES):
            if cc == c and r0 <= p0 and p0 + m <= r0 + n:
                copy.wait_recv()
        full = seen[c] + n == nbr
        contract(app_oth, accs[c], stages[c], e0, ne, r0, n, seen[c] == 0, full)
        seen[c] += n
        if full and c < LAST:
            meet(ne, stages[c], pairs[c], c).start()
        if i == 0:
            scatter(8, stage_own, pair_own, sb_own, rb_own, OWN)
        if i == 3:
            finish_own()
        if i == 5:
            rules()
        if full and c < LAST:
            scatter(ne, stages[c], pairs[c], *boxes[c], c)
        if i == 6:
            finish(0)
    e0, ne = CHUNKS[LAST]
    for q in range(4):
        at = pl.ds(q * PLANE // 4 * SEG, PLANE // 4 * SEG)
        sb3[at, :] = stage3[at, :].astype(BF16)

    @pl.when(mine)
    def _():
        scatter_last(ne, sb3, rb3, 1 - yh, PLANE, PLANE - 1, LAST)
        finish(LAST - 2)
        finish(LAST - 1)
        hop_own.wait_recv()
        sum_in[...] = sum_in[...] + sum_own[...]
        all_of(ne, sb3, rb3, 0, PLANE - 1, LAST).wait_send()

    @pl.when(theirs)
    def _():
        scatter_last(ne, sb3, rb3, yh, PLANE - 1, 0, LAST + 2)
        finish(LAST - 2)
        finish(LAST - 1)
        kept = e0 * SEG
        for copy in hops:
            copy.wait_recv()
        sum_in[pl.ds(0, kept), :] = sum_in[pl.ds(0, kept), :] + sum_oth[pl.ds(0, kept), :]
        rows = ne * SEG
        region = core * CHIPS + chip
        value = sb3[pl.ds(pl.multiple_of(region * rows, rows), rows), :].astype(F32)
        all_of(ne, sb3, rb3, 1, 0, LAST + 2).wait()
        for s in range(PLANE - 1):
            value = value + rb3[pl.ds(s * rows, rows), :].astype(F32)
        all_of(ne, sb3, rb3, 0, PLANE - 1, LAST).wait_recv()
        for s in range(PLANE - 1, 2 * PLANE - 1):
            value = value + rb3[pl.ds(s * rows, rows), :].astype(F32)
        sum_in[pl.ds(e0 * SEG, rows), :] = value

    value = sum_in[...]
    stage3[pl.ds(0, 8 * SEG), :] = jnp.where(mask[...] > 0.5, value * value, jnp.zeros_like(value))
    for t in range(SEG):
        out[:, t * 128:t * 128 + 128] = stage3[pl.ds(t, 8, stride=SEG), :]

    for copy in y_copies:
        copy.wait_send()

    @pl.when((b < last) & (b != low))
    def _():
        next_copy.wait_send()

    @pl.when((b > 0) & (b != high))
    def _():
        prev_copy.wait_send()

    @pl.when(at_low)
    def _():
        for copy in up_first:
            copy.wait_send()

    @pl.when(at_high)
    def _():
        for copy in down_first:
            copy.wait_send()

    for j in (1, 2, 3):
        @pl.when(b == high + UP + 2 * j)
        def _():
            up_second[j - 1].wait_send()
    for j in (0, 1, 2):
        @pl.when(b == 2 * j)
        def _():
            down_second[j].wait_send()

    @pl.when(mine)
    def _():
        for copy in hops:
            copy.wait_send()

    @pl.when(theirs)
    def _():
        hop_own.wait_send()


def on_device(bra, dipole, block_cols, ket, j_upper, sym_upper, j_lower, sym_lower):
    rows, upper = bra.shape
    half = ket.shape[1]
    nbr = rows // BLK
    hbm = pl.BlockSpec(memory_space=pl.ANY)
    dma = lambda n: pltpu.SemaphoreType.DMA((n,))
    box = lambda slots, ne: pltpu.VMEM((slots * ne * SEG, 128), BF16)
    boxes = []
    for ne in (8,) + tuple(ne for _, ne in CHUNKS[:LAST]):
        boxes += [box(CHIPS, ne), box(CHIPS - 1, ne)]
    boxes += [box(PLANE, CHUNKS[LAST][1]), box(2 * PLANE - 1, CHUNKS[LAST][1])]
    sums = pltpu.VMEM((8 * SEG, 128), F32)
    accs = [pltpu.VMEM((upper // NT, ne * PLANE, NT), F32) for ne in (8,) + tuple(ne for _, ne in CHUNKS)]
    sizes = (8,) + tuple(ne for _, ne in CHUNKS)
    stages = [pltpu.VMEM((PLANE * ne * SEG, 128), F32) for ne in sizes]
    pairs = [pltpu.VMEM((CHIPS * ne * SEG, 128), F32) for ne in sizes[:-1]]
    whole = pltpu.SMEM(j_lower.shape, jnp.int32)
    segments = pltpu.VMEM((upper // 128, 128), jnp.int32)
    flops = 2 * rows * 8 * BLK * half + 2 * rows * 2 * half * upper
    return pl.pallas_call(
        kernel,
        out_shape=jax.ShapeDtypeStruct((8, upper), F32),
        in_specs=[hbm] * 8,
        out_specs=pl.BlockSpec(memory_space=pltpu.VMEM),
        scratch_shapes=[
            pltpu.SMEM(block_cols.shape[::-1], jnp.int32), whole, whole, segments, segments,
            pltpu.VMEM((upper // NT, rows, NT), BF16),
            pltpu.VMEM(dipole.shape, BF16),
            pltpu.VMEM((nbr, BLK, half), BF16),
            pltpu.VMEM((nbr + 2 * REACH, BLK, half), BF16),
            pltpu.VMEM((REACH // 4, BLK, half), BF16),
            pltpu.VMEM((half, half), BF16),
            pltpu.VMEM((half, rows), BF16),
            pltpu.VMEM((half, rows), BF16),
            sums,
            *accs,
            *stages,
            *pairs,
            *boxes,
            sums, sums, sums,
            dma(5), dma(upper // NT), dma(len(STEPS)), dma(2), dma(2), dma(2), dma(4), dma(4),
            dma(len(PIECES)), dma(len(PIECES)), dma(LAST + 2), dma(LAST + 2), dma(LAST + 3), dma(LAST + 3), dma(LAST + 2), dma(LAST + 2),
            pltpu.SemaphoreType.REGULAR((2,)),
        ],
        compiler_params=pltpu.CompilerParams(
            collective_id=0, has_side_effects=True, vmem_limit_bytes=56 * 1024 * 1024
        ),
        cost_estimate=pl.CostEstimate(flops=flops, bytes_accessed=28 * 1024 * 1024, transcendentals=0),
    )(
        block_cols.T, j_lower, sym_lower,
        j_upper.reshape(upper // 128, 128), sym_upper.reshape(upper // 128, 128),
        bra, dipole, ket.reshape(nbr, BLK, half),
    )


def solution(mesh):
    return jax.shard_map(
        on_device,
        mesh=mesh,
        in_specs=(
            P("basis", "grp"),
            P("basis", None, None, None),
            P("basis", None),
            P("basis", "grp"),
            P("grp"),
            P("grp"),
            P(),
            P(),
        ),
        out_specs=P("basis", "grp"),
        check_vma=False,
    )
```

```python
import jax
import jax.numpy as jnp
from jax import lax
from jax.experimental import pallas as pl
from jax.experimental.pallas import tpu as pltpu
from jax.sharding import PartitionSpec as P

MESH = pl.DeviceIdType.MESH
F32 = jnp.float32
BF16 = jnp.bfloat16

REACH = 8
BLK = 128
PLANE = 32
LINE = 8
SEG = 16
NT = 512

CHIPS = PLANE // 2
SHIFTS = sorted(
    ((dx, dz) for dz in range(4) for dx in range(4) if dx or dz),
    key=lambda t: -min(t[0], 4 - t[0]) - min(t[1], 4 - t[1]),
)
PLACES = [(dx, dz, dc) for dx, dz in SHIFTS + [(0, 0)] for dc in (1, 0)]
CHUNKS = ((0, 4), (4, 2), (6, 1), (7, 1))
LAST = len(CHUNKS) - 1
PIECES = (
    (0, 8, 1), (0, 9, 3), (0, 12, 4), (0, 16, 4), (0, 20, 4), (1, 8, 16),
    (0, 0, 8), (0, 24, 8), (1, 0, 8), (1, 24, 8),
    (2, 8, 16), (2, 0, 8), (2, 24, 8),
    (3, 8, 16), (3, 0, 8), (3, 24, 6), (3, 30, 2),
)
ARRIVALS = (
    (0, 8, 16), (1, 8, 16), (0, 0, 8), (0, 24, 8), (1, 0, 8), (1, 24, 8),
    (2, 8, 16), (2, 0, 8), (2, 24, 8), (3, 8, 16), (3, 0, 8), (3, 24, 6), (3, 30, 2),
)
INNER = ((8, 1, (0,)), (9, 3, (1,)), (12, 4, (2,)), (16, 4, (3,)), (20, 4, (4, 5)))
OUTER = ((0, 4, ()), (4, 4, (6,)), (24, 4, ()), (28, 4, (7, 8, 9, 10, 11, 12, 13, 14, 15, 16)))
STEPS = INNER + OUTER
UP = 24


def kernel(
    cols_hbm, jl_hbm, sl_hbm, ju_hbm, su_hbm, bra_hbm, dip_hbm, ket_hbm, out,
    cols, jl, sl, ju, su,
    bra, dip, ket_own, ket_ext, relay, perm, app_own, app_oth, mask,
    acc_own, acc0, acc1, acc2, acc3,
    stage_own, stage0, stage1, stage2, stage3, pair_own, pair0, pair1, pair2,
    sb_own, rb_own, sb0, rb0, sb1, rb1, sb2, rb2, sb3, rb3,
    sum_own, sum_oth, sum_in,
    small_sem, bra_sem, dip_sem, ket_sem, halo_send, halo_recv, corner_send, corner_recv,
    y_send, y_recv, pair_send, pair_recv, a_send, a_recv, s_send, s_recv, round_sem,
):
    b = lax.axis_index("basis")
    g = lax.axis_index("grp")
    yh = b // PLANE
    me = b % PLANE
    nbr = dip_hbm.shape[0]
    last = 2 * PLANE - 1
    low, high = PLANE - 1, PLANE
    mine = yh == g
    theirs = yh != g
    across = ((1 - yh) * PLANE + me, g)
    partner = (b, 1 - g)

    def tell(sem, device):
        pl.semaphore_signal(sem, inc=1, device_id=device, device_id_type=MESH)

    small = [
        pltpu.make_async_copy(src, dst, small_sem.at[i])
        for i, (src, dst) in enumerate(((cols_hbm, cols), (jl_hbm, jl), (sl_hbm, sl), (ju_hbm, ju), (su_hbm, su)))
    ]
    ket_copies = [
        pltpu.make_async_copy(ket_hbm, ket_own, ket_sem.at[0]),
        pltpu.make_async_copy(ket_hbm, ket_ext.at[pl.ds(REACH, nbr)], ket_sem.at[1]),
    ]
    dip_copies = {}
    for i, (r0, n, _) in enumerate(STEPS):
        rows = pl.ds(r0, n)
        dip_copies[r0] = pltpu.make_async_copy(dip_hbm.at[rows], dip.at[rows], dip_sem.at[i])
    bra_copies = [
        pltpu.make_async_copy(bra_hbm.at[:, pl.ds(n * NT, NT)], bra.at[n], bra_sem.at[n])
        for n in range(bra.shape[0])
    ]
    small[0].start()
    dip_copies[STEPS[0][0]].start()
    ket_copies[0].start()

    barrier = pltpu.get_barrier_semaphore()
    tell(barrier, partner)
    tell(barrier, across)
    for s in range(1, LINE):
        tell(barrier, (yh * PLANE + (me ^ s), g))
    for s in range(1, PLANE // LINE):
        tell(barrier, (yh * PLANE + (me ^ (s * LINE)), g))

    for r0, _, _ in STEPS[1:4]:
        dip_copies[r0].start()
    ket_copies[1].start()
    for r0, _, _ in STEPS[4:]:
        dip_copies[r0].start()
    @pl.when(me > 0)
    def _():
        tell(barrier, (b - 1, g))

    @pl.when(me < low)
    def _():
        tell(barrier, (b + 1, g))

    at_low, at_high = b == low, b == high
    relays_up = [high + UP + 2 * j for j in (1, 2, 3)]
    relays_down = [2 * j for j in (0, 1, 2)]
    is_up = (b == relays_up[0]) | (b == relays_up[1]) | (b == relays_up[2])
    is_down = (b == relays_down[0]) | (b == relays_down[1]) | (b == relays_down[2])

    @pl.when(at_low)
    def _():
        for peer in [high] + relays_up + relays_down:
            tell(barrier, (peer, g))

    @pl.when(at_high)
    def _():
        for peer in [low] + relays_up + relays_down:
            tell(barrier, (peer, g))

    @pl.when(is_up | is_down)
    def _():
        tell(barrier, (low, g))
        tell(barrier, (high, g))

    size = perm.shape[0]
    place = lax.broadcasted_iota(jnp.int32, (size, size), 0)
    state = lax.broadcasted_iota(jnp.int32, (size, size), 1)
    region = place & (PLANE - 1)
    wanted = (2 * (region & (CHIPS - 1)) + region // CHIPS) * 8 + place // PLANE
    perm[...] = jnp.where(state == wanted, 1.0, 0.0).astype(BF16)

    def apply_rows(r0, n, ket, base):
        def one(i, carry):
            r = r0 + i
            top = ket.shape[0] - 1
            blocks = [ket[jnp.clip(cols[k, r] - base, 0, top)] for k in range(cols.shape[0])]
            row = jnp.concatenate([dip[r, k] for k in range(cols.shape[0])], axis=1)
            value = jnp.dot(row, jnp.concatenate(blocks, axis=0), preferred_element_type=F32)
            turned = lax.dot_general(
                perm[...], value.astype(BF16), (((1,), (1,)), ((), ())), preferred_element_type=F32
            )
            app_own[:, pl.ds(pl.multiple_of(r * BLK, BLK), BLK)] = turned.astype(BF16)
            return carry

        lax.fori_loop(0, n, one, 0)

    def to_next(dst):
        return pltpu.make_async_remote_copy(
            ket_hbm.at[pl.ds(nbr - REACH, REACH)], ket_ext.at[pl.ds(0, REACH)],
            halo_send.at[0], halo_recv.at[0], device_id=(dst, g), device_id_type=MESH,
        )

    def to_prev(dst):
        return pltpu.make_async_remote_copy(
            ket_hbm.at[pl.ds(0, REACH)], ket_ext.at[pl.ds(REACH + nbr, REACH)],
            halo_send.at[1], halo_recv.at[1], device_id=(dst, g), device_id_type=MESH,
        )

    next_copy, prev_copy = to_next(jnp.minimum(b + 1, last)), to_prev(jnp.maximum(b - 1, 0))
    quarter = REACH // 4

    def corner(src, dst, sem, device):
        return pltpu.make_async_remote_copy(
            src, dst, corner_send.at[sem], corner_recv.at[sem], device_id=(device, g), device_id_type=MESH
        )

    def ket_part(start, j):
        return ket_hbm.at[pl.ds(start + quarter * j, quarter)]

    def ext_part(start, j):
        return ket_ext.at[pl.ds(start + quarter * j, quarter)]

    up_first = [corner(ket_part(nbr - REACH, 0), ext_part(0, 0), 0, high)]
    up_first += [corner(ket_part(nbr - REACH, j), relay, j, high + UP + 2 * j) for j in (1, 2, 3)]
    up_second = [corner(relay, ext_part(0, j), j, high) for j in (1, 2, 3)]
    down_first = [corner(ket_part(0, 3), ext_part(REACH + nbr, 3), 3, low)]
    down_first += [corner(ket_part(0, j), relay, j, 2 * j) for j in (0, 1, 2)]
    down_second = [corner(relay, ext_part(REACH + nbr, j), j, low) for j in (0, 1, 2)]

    def relay_on():
        for j in (1, 2, 3):
            @pl.when(b == high + UP + 2 * j)
            def _():
                up_first[j].wait_recv()
                up_second[j - 1].start()
        for j in (0, 1, 2):
            @pl.when(b == 2 * j)
            def _():
                down_first[j + 1].wait_recv()
                down_second[j].start()

    def halo_wait():
        ket_copies[1].wait()

        @pl.when((b > 0) & (b != high))
        def _():
            next_copy.wait_recv()

        @pl.when((b < last) & (b != low))
        def _():
            prev_copy.wait_recv()

        @pl.when(at_high)
        def _():
            up_first[0].wait_recv()
            for copy in up_second:
                copy.wait_recv()

        @pl.when(at_low)
        def _():
            down_first[0].wait_recv()
            for copy in down_second:
                copy.wait_recv()

    y_copies = []
    for i, (c, r0, n) in enumerate(PIECES):
        e0, ne = CHUNKS[c]
        part = (pl.ds(e0 * PLANE, ne * PLANE), pl.ds(r0 * BLK, n * BLK))
        y_copies.append(
            pltpu.make_async_remote_copy(
                app_own.at[part], app_oth.at[part], y_send.at[i], y_recv.at[i],
                device_id=partner, device_id_type=MESH,
            )
        )

    def enter():
        many = jnp.where(at_low | at_high, 7, jnp.where(is_up | is_down, 2, 0))
        ends = jnp.where(me > 0, 1, 0) + jnp.where(me < low, 1, 0)
        pl.semaphore_wait(barrier, LINE + PLANE // LINE + ends + many)

        @pl.when((b < last) & (b != low))
        def _():
            next_copy.start()

        @pl.when((b > 0) & (b != high))
        def _():
            prev_copy.start()

        @pl.when(at_low)
        def _():
            for copy in up_first:
                copy.start()

        @pl.when(at_high)
        def _():
            for copy in down_first:
                copy.start()

    def apply_step(r0, n, ready, ket, base):
        dip_copies[r0].wait()
        apply_rows(r0, n, ket, base)
        if r0 == INNER[0][0]:
            enter()
        for k in ready:
            y_copies[k].start()

    def spread(value, stage, ne, first):
        for h in range(value.shape[1] // 128):
            for q in range(value.shape[0] // 8):
                e, o = q // (PLANE // 8), (q % (PLANE // 8)) * 8
                at = pl.ds(o * SEG * ne + e * SEG + first + h, 8, stride=SEG * ne)
                stage[at, :] = value[q * 8:q * 8 + 8, h * 128:h * 128 + 128]

    def contract(lhs, acc, stage, e0, ne, r0, n, begin, end):
        k = pl.ds(r0 * BLK, n * BLK)

        def one(t, carry):
            value = jnp.dot(
                lhs[pl.ds(e0 * PLANE, ne * PLANE), k], bra[t, k, :], preferred_element_type=F32
            )
            if not begin:
                value = value + acc[t]
            if end:
                spread(value, stage, ne, t * (NT // 128))
            else:
                acc[t] = value
            return carry

        if ne > 2:
            lax.fori_loop(0, bra.shape[0], one, 0)
        else:
            for t in range(bra.shape[0]):
                one(t, 0)

    core = me & 1
    chip = me // 2

    def meet(ne, stage, pair, sem):
        rows = CHIPS * ne * SEG
        theirs_at = pl.ds(pl.multiple_of((1 - core) * rows, rows), rows)
        return pltpu.make_async_remote_copy(
            stage.at[theirs_at], pair, pair_send.at[sem], pair_recv.at[sem],
            device_id=(b ^ 1, g), device_id_type=MESH,
        )

    def scatter(ne, stage, pair, sb, rb, sem):
        rows = ne * SEG
        meet(ne, stage, pair, sem).wait()

        def one(o, carry):
            at = pl.ds(pl.multiple_of(o * 4 * rows, 4 * rows), 4 * rows)
            own = pl.ds(pl.multiple_of(core * CHIPS * rows + o * 4 * rows, 4 * rows), 4 * rows)
            sb[at, :] = (stage[own, :] + pair[at, :]).astype(BF16)
            return carry

        lax.fori_loop(0, CHIPS // 4, one, 0)
        for slot, (dx, dz) in enumerate(SHIFTS):
            owner = (chip // 4 + dz) % 4 * 4 + (chip % 4 + dx) % 4
            pltpu.make_async_remote_copy(
                sb.at[pl.ds(pl.multiple_of(owner * rows, rows), rows)], rb.at[pl.ds(slot * rows, rows)],
                a_send.at[sem], a_recv.at[sem],
                device_id=(yh * PLANE + 2 * owner + core, g), device_id_type=MESH,
            ).start()

    def take(ne, sb, rb, sem, total, e0):
        rows = ne * SEG
        pltpu.make_async_remote_copy(
            sb.at[pl.ds(0, (CHIPS - 1) * rows)], rb, a_send.at[sem], a_recv.at[sem],
            device_id=partner, device_id_type=MESH,
        ).wait()
        add_up(ne, sb, chip, rb, CHIPS - 1, total, e0)

    def add_up(ne, sb, region, rb, slots, total, e0):
        rows = ne * SEG

        def one(s, value):
            return value + rb[pl.ds(pl.multiple_of(s * rows, rows), rows), :].astype(F32)

        value = sb[pl.ds(pl.multiple_of(region * rows, rows), rows), :].astype(F32)
        total[pl.ds(e0 * SEG, rows), :] = lax.fori_loop(0, slots, one, value)

    def scatter_last(ne, sb, rb, plane, count, slot, sem):
        rows = ne * SEG
        for s, (dx, dz, dc) in enumerate(PLACES[:count]):
            to_chip = (chip // 4 + dz) % 4 * 4 + (chip % 4 + dx) % 4
            to_core = core ^ dc
            region = to_core * CHIPS + to_chip
            pltpu.make_async_remote_copy(
                sb.at[pl.ds(pl.multiple_of(region * rows, rows), rows)], rb.at[pl.ds((slot + s) * rows, rows)],
                a_send.at[sem], a_recv.at[sem],
                device_id=(plane * PLANE + 2 * to_chip + to_core, g), device_id_type=MESH,
            ).start()

    def all_of(ne, sb, rb, begin, slot, sem):
        rows = ne * SEG
        return pltpu.make_async_remote_copy(
            sb.at[pl.ds(0, (PLANE - begin) * rows)], rb.at[pl.ds(slot * rows, (PLANE - begin) * rows)],
            a_send.at[sem], a_recv.at[sem], device_id=partner, device_id_type=MESH,
        )

    def hop(total, e0, ne, sem):
        part = pl.ds(e0 * SEG, ne * SEG)
        return pltpu.make_async_remote_copy(
            total.at[part], sum_in.at[part], s_send.at[sem], s_recv.at[sem],
            device_id=across, device_id_type=MESH,
        )

    OWN = LAST + 1
    hop_own = hop(sum_own, 0, 8, OWN)
    hops = [hop(sum_oth, e0, ne, c) for c, (e0, ne) in enumerate(CHUNKS[:LAST])]
    boxes = ((sb0, rb0), (sb1, rb1), (sb2, rb2))
    stages = (stage0, stage1, stage2, stage3)
    pairs = (pair0, pair1, pair2)

    def finish(c):
        e0, ne = CHUNKS[c]
        take(ne, *boxes[c], c, sum_oth, e0)

        @pl.when(mine)
        def _():
            hops[c].start()

    def main():
        small[0].wait()
        ket_copies[0].wait()
        for r0, n, ready in INNER:
            apply_step(r0, n, ready, ket_own, b * nbr)
            if r0 == INNER[0][0]:
                for copy in bra_copies:
                    copy.start()
                for copy in small[1:]:
                    copy.start()
            if r0 == INNER[1][0]:
                for s in range(1, PLANE // LINE):
                    tell(round_sem.at[0], (yh * PLANE + (me ^ (s * LINE)), g))
        relay_on()
        for copy in bra_copies:
            copy.wait()
        contract(app_own, acc_own, stage_own, 0, 8, REACH, nbr - 2 * REACH, True, False)
        pl.semaphore_wait(round_sem.at[0], PLANE // LINE - 1)
        tell(round_sem.at[1], across)
        halo_wait()
        for r0, n, ready in OUTER:
            apply_step(r0, n, ready, ket_ext, b * nbr - REACH)
        contract(app_own, acc_own, stage_own, 0, 8, 0, REACH, False, False)
        contract(app_own, acc_own, stage_own, 0, 8, nbr - REACH, REACH, False, True)
        meet(8, stage_own, pair_own, OWN).start()
        pl.semaphore_wait(round_sem.at[1], 1)

    main()

    def rules():
        for copy in small[1:]:
            copy.wait()
        for e in range(8):
            allowed = (jnp.abs(jl[8 * b + e] - ju[...]) <= 1) & (su[...] != sl[8 * b + e])
            mask[pl.ds(e * SEG, SEG), :] = jnp.where(allowed, 1.0, 0.0)

    def finish_own():
        take(8, sb_own, rb_own, OWN, sum_own, 0)

        @pl.when(theirs)
        def _():
            hop_own.start()

    accs = (acc0, acc1, acc2, acc3)
    seen = [0] * len(CHUNKS)
    for i, (c, r0, n) in enumerate(ARRIVALS):
        e0, ne = CHUNKS[c]
        for copy, (cc, p0, m) in zip(y_copies, PIECES):
            if cc == c and r0 <= p0 and p0 + m <= r0 + n:
                copy.wait_recv()
        full = seen[c] + n == nbr
        contract(app_oth, accs[c], stages[c], e0, ne, r0, n, seen[c] == 0, full)
        seen[c] += n
        if full and c < LAST:
            meet(ne, stages[c], pairs[c], c).start()
        if i == 0:
            scatter(8, stage_own, pair_own, sb_own, rb_own, OWN)
        if i == 3:
            finish_own()
        if i == 5:
            rules()
        if full and c < LAST:
            scatter(ne, stages[c], pairs[c], *boxes[c], c)
        if i == 6:
            finish(0)
    e0, ne = CHUNKS[LAST]
    for q in range(4):
        at = pl.ds(q * PLANE // 4 * SEG, PLANE // 4 * SEG)
        sb3[at, :] = stage3[at, :].astype(BF16)

    @pl.when(mine)
    def _():
        scatter_last(ne, sb3, rb3, 1 - yh, PLANE, PLANE - 1, LAST)
        finish(LAST - 2)
        finish(LAST - 1)
        hop_own.wait_recv()
        sum_in[...] = sum_in[...] + sum_own[...]
        all_of(ne, sb3, rb3, 0, PLANE - 1, LAST).wait_send()

    @pl.when(theirs)
    def _():
        scatter_last(ne, sb3, rb3, yh, PLANE - 1, 0, LAST + 2)
        finish(LAST - 2)
        finish(LAST - 1)
        kept = e0 * SEG
        for copy in hops:
            copy.wait_recv()
        sum_in[pl.ds(0, kept), :] = sum_in[pl.ds(0, kept), :] + sum_oth[pl.ds(0, kept), :]
        rows = ne * SEG
        region = core * CHIPS + chip
        value = sb3[pl.ds(pl.multiple_of(region * rows, rows), rows), :].astype(F32)
        all_of(ne, sb3, rb3, 1, 0, LAST + 2).wait()
        for s in range(PLANE - 1):
            value = value + rb3[pl.ds(s * rows, rows), :].astype(F32)
        all_of(ne, sb3, rb3, 0, PLANE - 1, LAST).wait_recv()
        for s in range(PLANE - 1, 2 * PLANE - 1):
            value = value + rb3[pl.ds(s * rows, rows), :].astype(F32)
        sum_in[pl.ds(e0 * SEG, rows), :] = value

    value = sum_in[...]
    stage3[pl.ds(0, 8 * SEG), :] = jnp.where(mask[...] > 0.5, value * value, jnp.zeros_like(value))
    for t in range(SEG):
        out[:, t * 128:t * 128 + 128] = stage3[pl.ds(t, 8, stride=SEG), :]

    for copy in y_copies:
        copy.wait_send()

    @pl.when((b < last) & (b != low))
    def _():
        next_copy.wait_send()

    @pl.when((b > 0) & (b != high))
    def _():
        prev_copy.wait_send()

    @pl.when(at_low)
    def _():
        for copy in up_first:
            copy.wait_send()

    @pl.when(at_high)
    def _():
        for copy in down_first:
            copy.wait_send()

    for j in (1, 2, 3):
        @pl.when(b == high + UP + 2 * j)
        def _():
            up_second[j - 1].wait_send()
    for j in (0, 1, 2):
        @pl.when(b == 2 * j)
        def _():
            down_second[j].wait_send()

    @pl.when(mine)
    def _():
        for copy in hops:
            copy.wait_send()

    @pl.when(theirs)
    def _():
        hop_own.wait_send()


def on_device(bra, dipole, block_cols, ket, j_upper, sym_upper, j_lower, sym_lower):
    rows, upper = bra.shape
    half = ket.shape[1]
    nbr = rows // BLK
    hbm = pl.BlockSpec(memory_space=pl.ANY)
    dma = lambda n: pltpu.SemaphoreType.DMA((n,))
    box = lambda slots, ne: pltpu.VMEM((slots * ne * SEG, 128), BF16)
    boxes = []
    for ne in (8,) + tuple(ne for _, ne in CHUNKS[:LAST]):
        boxes += [box(CHIPS, ne), box(CHIPS - 1, ne)]
    boxes += [box(PLANE, CHUNKS[LAST][1]), box(2 * PLANE - 1, CHUNKS[LAST][1])]
    sums = pltpu.VMEM((8 * SEG, 128), F32)
    accs = [pltpu.VMEM((upper // NT, ne * PLANE, NT), F32) for ne in (8,) + tuple(ne for _, ne in CHUNKS)]
    sizes = (8,) + tuple(ne for _, ne in CHUNKS)
    stages = [pltpu.VMEM((PLANE * ne * SEG, 128), F32) for ne in sizes]
    pairs = [pltpu.VMEM((CHIPS * ne * SEG, 128), F32) for ne in sizes[:-1]]
    whole = pltpu.SMEM(j_lower.shape, jnp.int32)
    segments = pltpu.VMEM((upper // 128, 128), jnp.int32)
    flops = 2 * rows * 8 * BLK * half + 2 * rows * 2 * half * upper
    return pl.pallas_call(
        kernel,
        out_shape=jax.ShapeDtypeStruct((8, upper), F32),
        in_specs=[hbm] * 8,
        out_specs=pl.BlockSpec(memory_space=pltpu.VMEM),
        scratch_shapes=[
            pltpu.SMEM(block_cols.shape[::-1], jnp.int32), whole, whole, segments, segments,
            pltpu.VMEM((upper // NT, rows, NT), BF16),
            pltpu.VMEM(dipole.shape, BF16),
            pltpu.VMEM((nbr, BLK, half), BF16),
            pltpu.VMEM((nbr + 2 * REACH, BLK, half), BF16),
            pltpu.VMEM((REACH // 4, BLK, half), BF16),
            pltpu.VMEM((half, half), BF16),
            pltpu.VMEM((half, rows), BF16),
            pltpu.VMEM((half, rows), BF16),
            sums,
            *accs,
            *stages,
            *pairs,
            *boxes,
            sums, sums, sums,
            dma(5), dma(upper // NT), dma(len(STEPS)), dma(2), dma(2), dma(2), dma(4), dma(4),
            dma(len(PIECES)), dma(len(PIECES)), dma(LAST + 2), dma(LAST + 2), dma(LAST + 3), dma(LAST + 3), dma(LAST + 2), dma(LAST + 2),
            pltpu.SemaphoreType.REGULAR((2,)),
        ],
        compiler_params=pltpu.CompilerParams(
            collective_id=0, has_side_effects=True, vmem_limit_bytes=56 * 1024 * 1024
        ),
        cost_estimate=pl.CostEstimate(flops=flops, bytes_accessed=28 * 1024 * 1024, transcendentals=0),
    )(
        block_cols.T, j_lower, sym_lower,
        j_upper.reshape(upper // 128, 128), sym_upper.reshape(upper // 128, 128),
        bra, dipole, ket.reshape(nbr, BLK, half),
    )


def solution(mesh):
    return jax.shard_map(
        on_device,
        mesh=mesh,
        in_specs=(
            P("basis", "grp"),
            P("basis", None, None, None),
            P("basis", None),
            P("basis", "grp"),
            P("grp"),
            P("grp"),
            P(),
            P(),
        ),
        out_specs=P("basis", "grp"),
        check_vma=False,
    )
```
